256 devices in a mesh: lon: 8 (over z), lat: 16 (over y, x), lev: 2 (over core).
Axes of the slice: x: 4, y: 4, z: 8, core: 2. Of those that a mesh axis runs over, the one named last changes fastest.
Arguments:
- ensemble: float32 [80, 3, 2, 256, 1024], P(None, None, 'lev', 'lat', 'lon'), may hold values from -6 to 6
- courant: float32 [2, 2, 256, 1024], P(None, 'lev', 'lat', 'lon'), may hold values from -0.6 to 0.6
- obs_value: float32 [2, 256], replicated, may hold values from -6 to 6
- obs_error: float32 [2, 256], replicated, may hold values from 0.25 to 4
- owner_device: int32 [2], replicated, may hold values from 0 to 255
- columns: int32 [2, 256], replicated, may hold values from 0 to 2047
Outputs:
- analysis: float32 [80, 3, 2, 256, 1024], P(None, None, 'lev', 'lat', 'lon')
The draws below stay inside these ranges and needn't reach their ends.
Inputs may be any that keep to these rules, and one draw needn't show every extreme that they name: `owner_device`: devices are counted over lon, lat and lev with lev fastest; all observations of a batch lie on the owner's level and observe the first field. `columns`: A column index counts the owner's cells row by row of 128 longitudes; two observations may share a column.
All inputs are finite; a program needn't handle non-finite values.
Results may differ from the reference program's by a relative error of at most 0.0003.
Values sent between devices are 32-bit elements; how exact they have to be, the bound alone decides.
A program may use at most 128 MiB of HBM per device.

```python
import math
import jax
import jax.numpy as jnp
from jax import lax

M = 80
VARS = 3
NOBS = 256
BATCHES = 2
CX = 128
CY = 16
LEVELS = 2
NLON = 1024
NLAT = 256
N_LON = 8
N_LAT = 16
N_LEV = 2


def touch_ends(drawn, stream_key, low, high):
    shape = drawn.shape
    index_at = [jax.random.randint(jax.random.fold_in(stream_key, axis), (), 0, shape[axis]) for axis in range(len(shape))]
    drawn = drawn.at[tuple(index_at)].set(low)
    longest = shape.index(max(shape))
    index_at[longest] = (index_at[longest] + 1) % shape[longest]
    return drawn.at[tuple(index_at)].set(high)


def block_scale(own_key, extent, split, smallest, top_value):
    level, own = 1.0, jax.random.fold_in(own_key, 6)
    for dim, blocks in split:
        heights = jnp.exp(jax.random.uniform(jax.random.fold_in(own, dim), (blocks,), jnp.float32, smallest / len(split), top_value / len(split)))
        level = level * jnp.repeat(heights, extent[dim] // blocks).reshape([-1 if axis == dim else 1 for axis in range(len(extent))])
    return level


def scatter_about(key, shape, scale, most, pieces=(), held_as=jnp.bfloat16):
    result = jax.random.normal(key, shape, jnp.float32) * scale
    if len(pieces) > 0:
        result = block_scale(key, shape, pieces, -0.22, 0.18) * result
    return jnp.clip(result, min=-most, max=most).astype(held_as)


def setup_inputs(seed: int = 0) -> dict:
    streams_of = jax.random.split(jax.random.key(seed), 7)
    ensemble = scatter_about(streams_of[0], (M, VARS, LEVELS, NLAT, NLON), 1.0, 6.0, ((2, 2), (3, 16), (4, 8)), jnp.float32)
    courant = jnp.clip(jax.random.uniform(streams_of[1], (2, LEVELS, NLAT, NLON), jnp.float32, -0.6, 0.6) * block_scale(streams_of[1], (2, LEVELS, NLAT, NLON), ((1, 2), (2, 16), (3, 8)), -0.4, 0.0), -0.6, 0.6)
    obs_value = scatter_about(streams_of[2], (BATCHES, NOBS), 1.0, 6.0, (), jnp.float32)
    obs_error = jnp.clip(jnp.exp(jax.random.uniform(streams_of[3], (BATCHES, NOBS), jnp.float32, math.log(0.25), math.log(4.0))), 0.25, 4.0)
    owner_device = jax.random.randint(streams_of[4], (BATCHES,), 0, N_LON * N_LAT * N_LEV).astype(jnp.int32)
    columns = touch_ends(jax.random.randint(streams_of[5], (BATCHES, NOBS), 0, CX * CY), jax.random.fold_in(streams_of[5], 1), 0, (CX * CY) - 1).astype(jnp.int32)
    return {"ensemble": ensemble, "courant": courant, "obs_value": obs_value, "obs_error": obs_error, "owner_device": owner_device, "columns": columns}


PLUS_WEIGHTS = (-2.0, 15.0, -60.0, 20.0, 30.0, -3.0)
MINUS_WEIGHTS = (3.0, -30.0, -20.0, 60.0, -15.0, 2.0)

def upwind(padded, along_axis, length_out):
    plus_sum = PLUS_WEIGHTS[0] * lax.slice_in_dim(padded, 0, length_out, axis=along_axis)
    minus_sum = MINUS_WEIGHTS[0] * lax.slice_in_dim(padded, 1, 1 + length_out, axis=along_axis)
    for offset_index in range(1, 6):
        plus_sum = plus_sum + PLUS_WEIGHTS[offset_index] * lax.slice_in_dim(padded, offset_index, offset_index + length_out, axis=along_axis)
        minus_sum = minus_sum + MINUS_WEIGHTS[offset_index] * lax.slice_in_dim(padded, offset_index + 1, offset_index + 1 + length_out, axis=along_axis)
    return (plus_sum / 60.0, minus_sum / 60.0)

def combine(plus_lon, minus_lon, plus_lat, minus_lat, east_courant, north_courant):
    lon_term = jnp.maximum(east_courant, 0.0) * plus_lon + jnp.minimum(east_courant, 0.0) * minus_lon
    lat_term = jnp.maximum(north_courant, 0.0) * plus_lat + jnp.minimum(north_courant, 0.0) * minus_lat
    return -(lon_term + lat_term)

def innovation_terms(obs_prior, observed, obs_err):
    members = obs_prior.shape[0]
    centre = lax.optimization_barrier(jnp.mean(obs_prior, axis=0))
    obs_spread = obs_prior - centre
    variance = lax.optimization_barrier(jnp.sum(obs_spread * obs_spread, axis=0)) / (members - 1)
    denominator = variance + obs_err
    factor = 1.0 / (1.0 + jnp.sqrt(obs_err / denominator))
    gain_matrix = (observed - centre - factor * obs_spread) / denominator
    return (obs_spread, gain_matrix)

def taper_tile(obs_rows, obs_cols, grid_rows, grid_cols, lon_total):
    dlat = (grid_rows[None, :, None] - obs_rows[:, None, None]).astype(jnp.float32)
    lon_gap = jnp.abs(grid_cols[None, None, :] - obs_cols[:, None, None])
    lon_gap = jnp.minimum(lon_gap, lon_total - lon_gap).astype(jnp.float32)
    ratio = jnp.sqrt((dlat / (2.0 * CY)) ** 2 + (lon_gap / (1.0 * (lon_total // 2))) ** 2)
    inner = -ratio ** 5 / 4.0 + ratio ** 4 / 2.0 + 5.0 * ratio ** 3 / 8.0 - 5.0 * ratio ** 2 / 3.0 + 1.0
    safe = jnp.maximum(ratio, 1.0)
    outer = safe ** 5 / 12.0 - safe ** 4 / 2.0 + 5.0 * safe ** 3 / 8.0 + 5.0 * safe ** 2 / 3.0 - 5.0 * safe + 4.0 - 2.0 / (3.0 * safe)
    return jnp.where(ratio <= 1.0, inner, jnp.where(ratio < 2.0, outer, 0.0)).astype(jnp.float32)

def advect_member(member, east_courant, north_courant):

    def tendency(values):
        lon_padded = jnp.concatenate([values[..., -3:], values, values[..., :3]], axis=3)
        lat_padded = jnp.pad(values, ((0, 0), (0, 0), (3, 3), (0, 0)))
        plus_lon, minus_lon = upwind(lon_padded, 3, NLON)
        plus_lat, minus_lat = upwind(lat_padded, 2, NLAT)
        return combine(plus_lon, minus_lon, plus_lat, minus_lat, east_courant, north_courant)
    section_one = member + tendency(member) / 3.0
    section_two = member + tendency(section_one) / 2.0
    return member + tendency(section_two)

def reference(ensemble, courant, obs_value, obs_error, owner_device, columns):
    members = ensemble.shape[0]
    field_count = ensemble.shape[1]
    levels = ensemble.shape[2]
    blocks = NLAT // CY
    analysis = ensemble
    for batch_index in range(BATCHES):
        device = owner_device[batch_index]
        lon_index = device // (N_LAT * N_LEV)
        lat_index = device // N_LEV % N_LAT
        lev_index = device % N_LEV
        row_ids = (lat_index * CY + columns[batch_index] // CX).astype(jnp.int32)
        col_ids = (lon_index * CX + columns[batch_index] % CX).astype(jnp.int32)
        level_field = analysis[:, 0][:, lev_index]
        obs_prior = level_field[:, row_ids, col_ids]
        obs_spread, gain_matrix = innovation_terms(obs_prior, obs_value[batch_index], obs_error[batch_index])
        centre = lax.optimization_barrier(jnp.mean(analysis, axis=0))
        anomaly = analysis - centre
        state_tiles = anomaly.reshape(members, field_count, levels, blocks, CY, NLON).transpose(2, 3, 0, 1, 4, 5)
        state_tiles = state_tiles.reshape(levels * blocks, members, field_count, CY, NLON)
        tile_ids = jnp.arange(levels * blocks, dtype=jnp.int32)
        grid_cols = jnp.arange(NLON, dtype=jnp.int32)

        def update_block(block_pair):
            block_state, tile_id = block_pair
            grid_rows = tile_id % blocks * CY + jnp.arange(CY, dtype=jnp.int32)
            block_weight = taper_tile(row_ids, col_ids, grid_rows, grid_cols, NLON)
            covariance = jnp.einsum('mk,mfrc->kfrc', obs_spread, block_state, precision=lax.Precision.HIGHEST) / (members - 1)
            weighted = block_weight[:, None] * covariance
            return jnp.einsum('mk,kfrc->mfrc', gain_matrix, weighted, precision=lax.Precision.HIGHEST)
        change = lax.map(update_block, (state_tiles, tile_ids))
        change = change.reshape(levels, blocks, members, field_count, CY, NLON).transpose(2, 3, 0, 1, 4, 5)
        analysis = analysis + change.reshape(analysis.shape)
    east_courant = courant[0]
    north_courant = courant[1]
    return lax.map(lambda member: advect_member(member, east_courant, north_courant), analysis)
```

```python
import functools

import jax
import jax.numpy as jnp
from jax import lax
from jax.experimental import pallas as pl
from jax.experimental.pallas import tpu as pltpu
from jax.sharding import PartitionSpec as P

MESH = pl.DeviceIdType.MESH
PLUS_WEIGHTS = (-2.0, 15.0, -60.0, 20.0, 30.0, -3.0)
MINUS_WEIGHTS = (3.0, -30.0, -20.0, 60.0, -15.0, 2.0)
VMEM_LIMIT = 60 * 1024 * 1024


def share_kernel(n_lon, n_lat, n_lev, cand, out, rs_buf, z_buf, send_sems, recv_sems):
    lon = lax.axis_index("lon")
    lat = lax.axis_index("lat")
    lev = lax.axis_index("lev")
    group = n_lat * n_lev
    me = lat * n_lev + lev

    def wait_all(buf, count, sem):
        view = buf.at[pl.ds(0, count)]
        pltpu.make_async_copy(view, view, sem).wait()

    def send_piece(t, carry):
        other = lax.rem(me + t, group)
        pltpu.make_async_remote_copy(
            src_ref=cand.at[other],
            dst_ref=rs_buf.at[me],
            send_sem=send_sems.at[0],
            recv_sem=recv_sems.at[0],
            device_id=(lon, other // n_lev, lax.rem(other, n_lev)),
            device_id_type=MESH,
        ).start()
        return carry

    lax.fori_loop(1, group, send_piece, 0)
    rs_buf[me] = cand[me]
    wait_all(rs_buf, group - 1, recv_sems.at[0])
    z_buf[lon] = jnp.sum(rs_buf[...], axis=0)

    def send_sum(t, carry):
        other = lax.rem(lon + t, n_lon)
        pltpu.make_async_remote_copy(
            src_ref=z_buf.at[lon],
            dst_ref=z_buf.at[lon],
            send_sem=send_sems.at[1],
            recv_sem=recv_sems.at[1],
            device_id=(other, lat, lev),
            device_id_type=MESH,
        ).start()
        return carry

    lax.fori_loop(1, n_lon, send_sum, 0)
    wait_all(z_buf, n_lon - 1, recv_sems.at[1])
    out[me] = jnp.sum(z_buf[...], axis=0)

    def send_total(t, carry):
        other = lax.rem(me + t, group)
        pltpu.make_async_remote_copy(
            src_ref=out.at[me],
            dst_ref=out.at[me],
            send_sem=send_sems.at[2],
            recv_sem=recv_sems.at[2],
            device_id=(lon, other // n_lev, lax.rem(other, n_lev)),
            device_id_type=MESH,
        ).start()
        return carry

    lax.fori_loop(1, group, send_total, 0)
    wait_all(out, group - 1, recv_sems.at[2])
    wait_all(rs_buf, group - 1, send_sems.at[0])
    wait_all(z_buf, n_lon - 1, send_sems.at[1])
    wait_all(out, group - 1, send_sems.at[2])


def share_prior(pieces, sizes):
    n_lon, n_lat, n_lev = sizes
    group, rows, lanes = pieces.shape
    return pl.pallas_call(
        functools.partial(share_kernel, n_lon, n_lat, n_lev),
        out_shape=jax.ShapeDtypeStruct(pieces.shape, jnp.float32),
        in_specs=[pl.BlockSpec(memory_space=pltpu.VMEM)],
        out_specs=pl.BlockSpec(memory_space=pltpu.VMEM),
        scratch_shapes=[
            pltpu.VMEM((group, rows, lanes), jnp.float32),
            pltpu.VMEM((n_lon, rows, lanes), jnp.float32),
            pltpu.SemaphoreType.DMA((3,)),
            pltpu.SemaphoreType.DMA((3,)),
        ],
        compiler_params=pltpu.CompilerParams(
            has_side_effects=True, vmem_limit_bytes=16 * 1024 * 1024
        ),
        name="share_prior",
    )(pieces)


def split(x):
    hi = x.astype(jnp.bfloat16)
    lo = (x - hi.astype(jnp.float32)).astype(jnp.bfloat16)
    return hi, lo


def taper_of(r2):
    inv = lax.rsqrt(jnp.maximum(r2, 1e-30))
    r = r2 * inv
    inner = 1.0 + r2 * (-5.0 / 3.0 + r * (0.625 + r * (0.5 - 0.25 * r)))
    outer = (
        4.0
        - (2.0 / 3.0) * inv
        + r * (-5.0 + r * (5.0 / 3.0 + r * (0.625 + r * (-0.5 + r * (1.0 / 12.0)))))
    )
    return jnp.where(r2 <= 1.0, inner, jnp.where(r2 < 4.0, outer, 0.0))


def dot(a, b):
    return jnp.dot(a, b, preferred_element_type=jnp.float32)


def innovation(prior, value, err):
    members = prior.shape[0]
    centre = jnp.sum(prior, axis=0, keepdims=True) * (1.0 / members)
    spread = prior - centre
    variance = jnp.sum(spread * spread, axis=0, keepdims=True) * (1.0 / (members - 1))
    denominator = variance + err
    factor = 1.0 / (1.0 + jnp.sqrt(err / denominator))
    gain = (value - centre - factor * spread) / denominator
    return spread, gain


def spread_operand(spread):
    members, count = spread.shape
    hi, lo = split(spread * (1.0 / (members - 1)))
    pad = jnp.zeros((256 - 3 * members, count), jnp.float32)
    stacked = jnp.concatenate(
        [hi.astype(jnp.float32), lo.astype(jnp.float32), hi.astype(jnp.float32), pad], axis=0
    )
    return stacked.T.astype(jnp.bfloat16)


def anomaly_operand(x):
    members = x.shape[0]
    a = x - jnp.sum(x, axis=0, keepdims=True) * (1.0 / members)
    hi, lo = split(a)
    pad = jnp.zeros((256 - 3 * members, x.shape[1]), jnp.bfloat16)
    return jnp.concatenate([hi, hi, lo, pad], axis=0)


def apply_gain(gain_stack, gain_hi, weighted):
    members = gain_hi.shape[0]
    hi, lo = split(weighted)
    both = dot(gain_stack, hi)
    return both[:members] + both[members:] + dot(gain_hi, lo)


def assimilate_kernel(
    lat_rows, members, fields,
    x_ref, prior_ref, value_ref, err_ref, rowk_ref, colk_ref, rowl_ref, coll_ref, out_ref,
    s_op, g_op, lon_part, row_part,
):
    cols = x_ref.shape[-1]
    lat0 = lax.axis_index("lat") * lat_rows
    lon0 = lax.axis_index("lon") * cols
    n_total = cols * lax.axis_size("lon")
    batches, _, count = prior_ref.shape

    def lon_sq(gap):
        gap = jnp.abs(gap)
        gap = jnp.minimum(gap, n_total - gap).astype(jnp.float32) * (1.0 / (n_total // 2))
        return gap * gap

    prior = prior_ref[0]
    for b in range(batches):
        spread, gain = innovation(prior, value_ref[b : b + 1], err_ref[b : b + 1])
        s_op[b] = spread_operand(spread)
        ghi, glo = split(gain)
        g_op[b] = jnp.concatenate([ghi, glo], axis=0)
        grid_cols = lon0 + lax.broadcasted_iota(jnp.int32, (count, cols), 1)
        lon_part[b] = lon_sq(grid_cols - colk_ref[b])
        row_part[b] = jnp.broadcast_to(rowk_ref[b].astype(jnp.float32), (count, cols))
        if b + 1 < batches:
            prior = prior_ref[b + 1]
            dlat = (rowl_ref[b + 1 : b + 2] - rowk_ref[b]).astype(jnp.float32) * (1.0 / 32.0)
            taper = taper_of(dlat * dlat + lon_sq(coll_ref[b + 1 : b + 2] - colk_ref[b]))
            cov = dot(s_op[b], anomaly_operand(prior))
            prior = prior + apply_gain(g_op[b], ghi, taper * cov)

    def row_step(i, carry):
        x = [x_ref[i, f] for f in range(fields)]
        lat = (lat0 + i).astype(jnp.float32)
        for b in range(batches):
            dlat = (lat - row_part[b]) * (1.0 / 32.0)
            taper = taper_of(dlat * dlat + lon_part[b])
            operand = jnp.concatenate([anomaly_operand(v) for v in x], axis=1)
            cov = dot(s_op[b], operand)
            weighted = jnp.concatenate(
                [taper * cov[:, f * cols : (f + 1) * cols] for f in range(fields)], axis=1
            )
            change = apply_gain(g_op[b], g_op[b, :members], weighted)
            x = [x[f] + change[:, f * cols : (f + 1) * cols] for f in range(fields)]
        for f in range(fields):
            out_ref[i, f] = x[f]
        return carry

    lax.fori_loop(0, lat_rows, row_step, 0)


def assimilate(x, prior, obs_value, obs_error, obs_rows, obs_cols):
    lat_rows, fields, members, cols = x.shape
    batches, _, count = prior.shape
    vmem = pl.BlockSpec(memory_space=pltpu.VMEM)
    return pl.pallas_call(
        functools.partial(assimilate_kernel, lat_rows, members, fields),
        out_shape=jax.ShapeDtypeStruct(x.shape, jnp.float32),
        in_specs=[vmem] * 8,
        out_specs=vmem,
        scratch_shapes=[
            pltpu.VMEM((batches, count, 256), jnp.bfloat16),
            pltpu.VMEM((batches, 2 * members, count), jnp.bfloat16),
            pltpu.VMEM((batches, count, cols), jnp.float32),
            pltpu.VMEM((batches, count, cols), jnp.float32),
        ],
        compiler_params=pltpu.CompilerParams(vmem_limit_bytes=VMEM_LIMIT),
        name="assimilate",
    )(
        x, prior, obs_value, obs_error,
        obs_rows[:, :, None], obs_cols[:, :, None], obs_rows, obs_cols,
    )


WIDTH = 3
SUB = 8


def advect_kernel(
    n_lon, n_lat,
    x_ref, cour_ref, out_ref,
    state, packed, left_in, right_in, fix, coef, edge_coef,
    lat_send, lat_recv, lon_send, lon_recv,
):
    rows, count, cols = x_ref.shape
    lon = lax.axis_index("lon")
    lat = lax.axis_index("lat")
    lev = lax.axis_index("lev")
    has_up = lat > 0
    has_down = lat < n_lat - 1
    east = lax.rem(lon + 1, n_lon)
    west = lax.rem(lon + n_lon - 1, n_lon)
    lane = lax.broadcasted_iota(jnp.int32, (SUB, cols), 1)
    groups = count // SUB
    slot = 2 * WIDTH
    edge_lane = (lane < WIDTH) | (lane >= cols - WIDTH)
    from_left = lax.rem(lane, slot) < WIDTH

    def lat_copy(section, down):
        src = rows if down else WIDTH
        dst = 0 if down else WIDTH + rows
        return pltpu.make_async_remote_copy(
            src_ref=state.at[section, pl.ds(src, WIDTH)],
            dst_ref=state.at[section, pl.ds(dst, WIDTH)],
            send_sem=lat_send.at[section, int(down)],
            recv_sem=lat_recv.at[section, int(down)],
            device_id=(lon, lat + 1 if down else lat - 1, lev),
            device_id_type=MESH,
        )

    def lon_copy(section, to_east):
        return pltpu.make_async_remote_copy(
            src_ref=packed.at[section],
            dst_ref=(left_in if to_east else right_in).at[section],
            send_sem=lon_send.at[section, int(to_east)],
            recv_sem=lon_recv.at[section, int(to_east)],
            device_id=(east if to_east else west, lat, lev),
            device_id_type=MESH,
        )

    state[0, WIDTH : WIDTH + rows] = x_ref[...]

    @pl.when(has_up)
    def _():
        lat_copy(0, False).start()

    @pl.when(has_down)
    def _():
        lat_copy(0, True).start()

    @pl.when(jnp.logical_not(has_up))
    def _():
        for s in range(3):
            state[s, 0:WIDTH] = jnp.zeros((WIDTH, count, cols), jnp.float32)

    @pl.when(jnp.logical_not(has_down))
    def _():
        for s in range(3):
            state[s, rows + WIDTH :] = jnp.zeros((WIDTH, count, cols), jnp.float32)

    def pack(section):
        def step(g, carry):
            sl = pl.ds(pl.multiple_of(g * SUB, SUB), SUB)
            acc = jnp.zeros((SUB, cols), jnp.float32)
            for r in range(rows):
                rolled = pltpu.roll(state[section, WIDTH + r, sl], WIDTH + slot * r, 1)
                keep = (lane >= slot * r) & (lane < slot * (r + 1))
                acc = jnp.where(keep, rolled, acc)
            packed[section, sl] = acc
            return carry

        lax.fori_loop(0, groups, step, 0, unroll=5)

    for r in range(rows):
        centre = None
        for d in range(2):
            c = jnp.broadcast_to(cour_ref[d, r : r + 1], (SUB, cols))
            up = jnp.maximum(c, 0.0) * (-1.0 / 60.0)
            dn = jnp.minimum(c, 0.0) * (-1.0 / 60.0)
            for o in range(7):
                w = PLUS_WEIGHTS[o] * up if o < 6 else jnp.zeros_like(c)
                if o > 0:
                    w = w + MINUS_WEIGHTS[o - 1] * dn
                if o == 3:
                    centre = w if d == 0 else centre + w
                else:
                    coef[r, d * 7 + o] = w
        coef[r, 3] = centre
    for o in (1, 2, 3):
        left = jnp.zeros((SUB, cols), jnp.float32)
        right = jnp.zeros((SUB, cols), jnp.float32)
        for r in range(rows):
            mid = slot * r + WIDTH
            left = jnp.where(
                (lane >= mid) & (lane < mid + o), pltpu.roll(coef[r, 3 - o], mid, 1), left
            )
            right = jnp.where(
                (lane >= mid - o) & (lane < mid), pltpu.roll(coef[r, 3 + o], mid, 1), right
            )
        edge_coef[0, o - 1] = left
        edge_coef[1, o - 1] = right

    for section in range(3):
        scale = (1.0 / 3.0, 0.5, 1.0)[section]
        pack(section)
        lon_copy(section, True).start()
        lon_copy(section, False).start()
        lon_copy(section, True).wait_recv()
        lon_copy(section, False).wait_recv()

        def fix_step(g, carry):
            sl = pl.ds(pl.multiple_of(g * SUB, SUB), SUB)
            d = jnp.where(from_left, left_in[section, sl], right_in[section, sl])
            d = d - packed[section, sl]
            t = edge_coef[0, 0] * pltpu.roll(d, 1, 1) + edge_coef[1, 0] * pltpu.roll(d, cols - 1, 1)
            for o in (2, 3):
                t = t + edge_coef[0, o - 1] * pltpu.roll(d, o, 1)
                t = t + edge_coef[1, o - 1] * pltpu.roll(d, cols - o, 1)
            fix[sl] = t
            return carry

        lax.fori_loop(0, groups, fix_step, 0, unroll=5)

        def do_row(r, carry):
            shift = lax.rem(2 * cols - WIDTH - slot * r, cols)
            w = [coef[r, o] if o != 10 else None for o in range(14)]
            for g in range(groups):
                sl = pl.ds(g * SUB, SUB)
                q = state[section, WIDTH + r, sl]
                t = w[3] * q
                u = jnp.where(edge_lane, pltpu.roll(fix[sl], shift, 1), 0.0)
                for o in (1, 2, 3):
                    t = t + w[3 - o] * pltpu.roll(q, o, 1)
                    u = u + w[3 + o] * pltpu.roll(q, cols - o, 1)
                    t = t + w[10 - o] * state[section, WIDTH + r - o, sl]
                    u = u + w[10 + o] * state[section, WIDTH + r + o, sl]
                base = q if section == 0 else state[0, WIDTH + r, sl]
                value = base + (t + u) * scale if section < 2 else base + (t + u)
                if section < 2:
                    state[section + 1, WIDTH + r, sl] = value
                else:
                    out_ref[r, sl] = value
            return carry

        lax.fori_loop(WIDTH, rows - WIDTH, do_row, 0)

        @pl.when(has_up)
        def _():
            lat_copy(section, True).wait_recv()

        @pl.when(has_down)
        def _():
            lat_copy(section, False).wait_recv()

        lax.fori_loop(0, WIDTH, do_row, 0)
        if section < 2:

            @pl.when(has_up)
            def _():
                lat_copy(section + 1, False).start()

        lax.fori_loop(rows - WIDTH, rows, do_row, 0)
        if section < 2:

            @pl.when(has_down)
            def _():
                lat_copy(section + 1, True).start()

    for section in range(3):
        lon_copy(section, True).wait_send()
        lon_copy(section, False).wait_send()

        @pl.when(has_up)
        def _():
            lat_copy(section, False).wait_send()

        @pl.when(has_down)
        def _():
            lat_copy(section, True).wait_send()


def advect(x, courant, sizes):
    n_lon, n_lat, _ = sizes
    rows, count, cols = x.shape
    vmem = pl.BlockSpec(memory_space=pltpu.VMEM)
    return pl.pallas_call(
        functools.partial(advect_kernel, n_lon, n_lat),
        out_shape=jax.ShapeDtypeStruct(x.shape, jnp.float32),
        in_specs=[vmem] * 2,
        out_specs=vmem,
        scratch_shapes=[
            pltpu.VMEM((3, rows + 2 * WIDTH, count, cols), jnp.float32),
            pltpu.VMEM((3, count, cols), jnp.float32),
            pltpu.VMEM((3, count, cols), jnp.float32),
            pltpu.VMEM((3, count, cols), jnp.float32),
            pltpu.VMEM((count, cols), jnp.float32),
            pltpu.VMEM((rows, 14, SUB, cols), jnp.float32),
            pltpu.VMEM((2, WIDTH, SUB, cols), jnp.float32),
            pltpu.SemaphoreType.DMA((3, 2)),
            pltpu.SemaphoreType.DMA((3, 2)),
            pltpu.SemaphoreType.DMA((3, 2)),
            pltpu.SemaphoreType.DMA((3, 2)),
        ],
        compiler_params=pltpu.CompilerParams(has_side_effects=True, vmem_limit_bytes=VMEM_LIMIT),
        name="advect",
    )(x, courant)


def on_device(ensemble, courant, obs_value, obs_error, owner_device, columns):
    members, fields, _, lat_rows, cols = ensemble.shape
    sizes = tuple(lax.axis_size(a) for a in ("lon", "lat", "lev"))
    n_lon, n_lat, n_lev = sizes
    batches, count = columns.shape
    lon_index = owner_device // (n_lat * n_lev)
    lat_index = owner_device // n_lev % n_lat
    obs_rows = lat_index[:, None] * lat_rows + columns // cols
    obs_cols = lon_index[:, None] * cols + columns % cols
    me = (lax.axis_index("lon") * n_lat + lax.axis_index("lat")) * n_lev + lax.axis_index("lev")

    first = ensemble[:, 0, 0].reshape(members, lat_rows * cols)
    cand = jnp.take(first, columns.reshape(-1), axis=1).reshape(members, batches, count)
    cand = jnp.where((owner_device == me)[None, :, None], cand, 0.0)
    group = n_lat * n_lev
    pieces = cand.reshape(group, members * batches * count // (group * 128), 128)
    prior = share_prior(pieces, sizes).reshape(members, batches, count).transpose(1, 0, 2)

    x = ensemble[:, :, 0].transpose(2, 1, 0, 3)
    x = assimilate(x, prior, obs_value, obs_error, obs_rows, obs_cols)
    x = x.reshape(lat_rows, fields * members, cols)
    x = advect(x, courant[:, 0], sizes)
    x = x.reshape(lat_rows, fields, members, cols).transpose(2, 1, 0, 3)
    return x[:, :, None]


def solution(mesh):
    return jax.shard_map(
        on_device,
        mesh=mesh,
        in_specs=(
            P(None, None, "lev", "lat", "lon"),
            P(None, "lev", "lat", "lon"),
            P(),
            P(),
            P(),
            P(),
        ),
        out_specs=P(None, None, "lev", "lat", "lon"),
        check_vma=False,
    )
```

```python
import functools

import jax
import jax.numpy as jnp
from jax import lax
from jax.experimental import pallas as pl
from jax.experimental.pallas import tpu as pltpu
from jax.sharding import PartitionSpec as P

MESH = pl.DeviceIdType.MESH
PLUS_WEIGHTS = (-2.0, 15.0, -60.0, 20.0, 30.0, -3.0)
MINUS_WEIGHTS = (3.0, -30.0, -20.0, 60.0, -15.0, 2.0)
VMEM_LIMIT = 60 * 1024 * 1024
WIDTH = 3
SUB = 8
ROWS = 4
LANES = 128


def split(x):
    hi = x.astype(jnp.bfloat16)
    lo = (x - hi.astype(jnp.float32)).astype(jnp.bfloat16)
    return hi, lo


def taper_of(r2):
    inv = lax.rsqrt(jnp.maximum(r2, 1e-30))
    r = r2 * inv
    inner = 1.0 + r2 * (-5.0 / 3.0 + r * (0.625 + r * (0.5 - 0.25 * r)))
    outer = (
        4.0
        - (2.0 / 3.0) * inv
        + r * (-5.0 + r * (5.0 / 3.0 + r * (0.625 + r * (-0.5 + r * (1.0 / 12.0)))))
    )
    return jnp.where(r2 <= 1.0, inner, jnp.where(r2 < 4.0, outer, 0.0))


def dot(a, b):
    return jnp.dot(a, b, preferred_element_type=jnp.float32)


def innovation(prior, value, err):
    members = prior.shape[0]
    centre = jnp.sum(prior, axis=0, keepdims=True) * (1.0 / members)
    spread = prior - centre
    variance = jnp.sum(spread * spread, axis=0, keepdims=True) * (1.0 / (members - 1))
    denominator = variance + err
    factor = 1.0 / (1.0 + jnp.sqrt(err / denominator))
    gain = (value - centre - factor * spread) / denominator
    return spread, gain


def spread_operand(spread):
    members, count = spread.shape
    hi, lo = split(spread * (1.0 / (members - 1)))
    pad = jnp.zeros((256 - 3 * members, count), jnp.float32)
    stacked = jnp.concatenate(
        [hi.astype(jnp.float32), lo.astype(jnp.float32), hi.astype(jnp.float32), pad], axis=0
    )
    return stacked.T.astype(jnp.bfloat16)


def anomaly_operand(x):
    members = x.shape[0]
    a = x - jnp.sum(x, axis=0, keepdims=True) * (1.0 / members)
    hi, lo = split(a)
    pad = jnp.zeros((256 - 3 * members, x.shape[1]), jnp.bfloat16)
    return jnp.concatenate([hi, hi, lo, pad], axis=0)


def apply_gain(gain_stack, gain_hi, weighted):
    members = gain_hi.shape[0]
    hi, lo = split(weighted)
    both = dot(gain_stack, hi)
    return both[:members] + both[members:] + dot(gain_hi, lo)


def kernel(
    dims,
    x_ref, cour_ref, value_ref, err_ref, local_ref, rowk_ref, colk_ref, rowl_ref, coll_ref, out_ref,
    cand, peer, mine, rs_buf, z_buf, full, prior_buf,
    s_op, g_op, lon_part, row_part, taper_buf,
    state, packed, left_in, right_in, fix, coef, edge_coef,
    share_send, share_recv, lat_send, lat_recv, lon_send, lon_recv,
):
    n_lon, n_lat, n_lev = dims
    rows, fields, members, cols = x_ref.shape
    batches, count = value_ref.shape
    total = fields * members
    lon = lax.axis_index("lon")
    lat = lax.axis_index("lat")
    lev = lax.axis_index("lev")
    has_up = lat > 0
    has_down = lat < n_lat - 1
    east = lax.rem(lon + 1, n_lon)
    west = lax.rem(lon + n_lon - 1, n_lon)
    other_lev = 1 - lev
    slot = 2 * WIDTH
    per = members // n_lat

    barrier = pltpu.get_barrier_semaphore()

    def greet_lat(t, carry):
        pl.semaphore_signal(
            barrier, inc=1, device_id=(lon, lax.rem(lat + t, n_lat), lev), device_id_type=MESH
        )
        return carry

    def greet_lon(t, carry):
        pl.semaphore_signal(
            barrier, inc=1, device_id=(lax.rem(lon + t, n_lon), lat, lev), device_id_type=MESH
        )
        return carry

    pl.semaphore_signal(barrier, inc=1, device_id=(lon, lat, other_lev), device_id_type=MESH)
    lax.fori_loop(1, n_lat, greet_lat, 0)
    lax.fori_loop(1, n_lon, greet_lon, 0)

    picked = None
    for pair in range(rows // 2):
        parts = [x_ref[2 * pair + j, 0] for j in range(2)]
        x0 = jnp.concatenate(parts, axis=1)
        hi = x0.astype(jnp.bfloat16)
        rest = x0 - hi.astype(jnp.float32)
        mid, lo = split(rest)
        cell = lax.broadcasted_iota(jnp.int32, (2 * cols, count), 0) + pair * 2 * cols
        hot = [
            jnp.where(cell == local_ref[b : b + 1], 1.0, 0.0).astype(jnp.bfloat16)
            for b in range(batches)
        ]
        term = dot(jnp.concatenate([hi, mid, lo], axis=0), jnp.concatenate(hot, axis=1))
        picked = term if picked is None else picked + term
    picked = picked[:members] + (picked[members : 2 * members] + picked[2 * members :])
    halves = count // LANES
    for b in range(batches):
        for p in range(n_lat):
            for h in range(halves):
                at = b * count + h * LANES
                cand[b, p, h * per : (h + 1) * per] = picked[p * per : (p + 1) * per, at : at + LANES]

    pl.semaphore_wait(barrier, n_lat + n_lon - 1)

    def wait_all(buf, number, sem):
        view = buf.at[pl.ds(0, number)]
        pltpu.make_async_copy(view, view, sem).wait()

    def swap_cand():
        return pltpu.make_async_remote_copy(
            src_ref=cand.at[other_lev], dst_ref=peer,
            send_sem=share_send.at[0], recv_sem=share_recv.at[0],
            device_id=(lon, lat, other_lev), device_id_type=MESH,
        )

    def send_piece(t, carry):
        other = lax.rem(lat + t, n_lat)
        pltpu.make_async_remote_copy(
            src_ref=mine.at[other], dst_ref=rs_buf.at[lat],
            send_sem=share_send.at[1], recv_sem=share_recv.at[1],
            device_id=(lon, other, lev), device_id_type=MESH,
        ).start()
        return carry

    def send_sum(t, carry):
        pltpu.make_async_remote_copy(
            src_ref=z_buf.at[lon], dst_ref=z_buf.at[lon],
            send_sem=share_send.at[2], recv_sem=share_recv.at[2],
            device_id=(lax.rem(lon + t, n_lon), lat, lev), device_id_type=MESH,
        ).start()
        return carry

    def send_total(t, carry):
        pltpu.make_async_remote_copy(
            src_ref=full.at[lev, lat], dst_ref=full.at[lev, lat],
            send_sem=share_send.at[3], recv_sem=share_recv.at[3],
            device_id=(lon, lax.rem(lat + t, n_lat), lev), device_id_type=MESH,
        ).start()
        return carry

    def swap_full():
        return pltpu.make_async_remote_copy(
            src_ref=full.at[lev], dst_ref=full.at[lev],
            send_sem=share_send.at[4], recv_sem=share_recv.at[4],
            device_id=(lon, lat, other_lev), device_id_type=MESH,
        )

    lat0 = lat * rows
    lon0 = lon * cols
    n_total = cols * n_lon

    def lon_sq(gap):
        gap = jnp.abs(gap)
        gap = jnp.minimum(gap, n_total - gap).astype(jnp.float32) * (1.0 / (n_total // 2))
        return gap * gap

    def tapers(first, last):
        def one(n, carry):
            b = n // rows
            i = lax.rem(n, rows)
            here = (lat0 + i).astype(jnp.float32)
            for at in range(0, count, 64):
                sl = pl.ds(at, 64)
                dlat = (here - row_part[b, sl]) * (1.0 / (2.0 * rows))
                taper_buf[b, i, sl] = taper_of(dlat * dlat + lon_part[b, sl])
            return carry

        lax.fori_loop(first, last, one, 0)

    swap_cand().start()
    for b in range(batches):
        grid_cols = lon0 + lax.broadcasted_iota(jnp.int32, (count, cols), 1)
        lon_part[b] = lon_sq(grid_cols - colk_ref[b])
        row_part[b] = jnp.broadcast_to(rowk_ref[b].astype(jnp.float32), (count, cols))
    swap_cand().wait_recv()
    for p in range(n_lat):
        mine[p] = cand[lev, p] + peer[p]
    lax.fori_loop(1, n_lat, send_piece, 0)
    rs_buf[lat] = mine[lat]
    tapers(0, 12)
    wait_all(rs_buf, n_lat - 1, share_recv.at[1])
    z_buf[lon] = jnp.sum(rs_buf[...], axis=0)
    lax.fori_loop(1, n_lon, send_sum, 0)
    tapers(12, 22)
    wait_all(z_buf, n_lon - 1, share_recv.at[2])
    full[lev, lat] = jnp.sum(z_buf[...], axis=0)
    lax.fori_loop(1, n_lat, send_total, 0)
    tapers(22, 2 * rows)
    wait_all(full.at[lev], n_lat - 1, share_recv.at[3])
    swap_full().start()

    lane = lax.broadcasted_iota(jnp.int32, (SUB, cols), 1)
    edge_lane = (lane < WIDTH) | (lane >= cols - WIDTH)
    from_left = lax.rem(lane, slot) < WIDTH
    for r in range(rows):
        centre = None
        for d in range(2):
            c = jnp.broadcast_to(cour_ref[d, r : r + 1], (SUB, cols))
            up = jnp.maximum(c, 0.0) * (-1.0 / 60.0)
            dn = jnp.minimum(c, 0.0) * (-1.0 / 60.0)
            for o in range(7):
                w = PLUS_WEIGHTS[o] * up if o < 6 else jnp.zeros_like(c)
                if o > 0:
                    w = w + MINUS_WEIGHTS[o - 1] * dn
                if o == 3:
                    centre = w if d == 0 else centre + w
                else:
                    coef[r, d * 7 + o] = w
        coef[r, 3] = centre
    for o in (1, 2, 3):
        left = jnp.zeros((SUB, cols), jnp.float32)
        right = jnp.zeros((SUB, cols), jnp.float32)
        for r in range(rows):
            mid = slot * r + WIDTH
            left = jnp.where(
                (lane >= mid) & (lane < mid + o), pltpu.roll(coef[r, 3 - o], mid, 1), left
            )
            right = jnp.where(
                (lane >= mid - o) & (lane < mid), pltpu.roll(coef[r, 3 + o], mid, 1), right
            )
        edge_coef[0, o - 1] = left
        edge_coef[1, o - 1] = right

    @pl.when(jnp.logical_not(has_up))
    def _():
        for s in range(3):
            state[s, 0:WIDTH] = jnp.zeros((WIDTH, total, cols), jnp.float32)

    @pl.when(jnp.logical_not(has_down))
    def _():
        for s in range(3):
            state[s, rows + WIDTH :] = jnp.zeros((WIDTH, total, cols), jnp.float32)

    swap_full().wait_recv()
    for b in range(batches):
        for p in range(n_lat):
            for h in range(halves):
                at = h * LANES
                prior_buf[b, p * per : (p + 1) * per, at : at + LANES] = full[
                    b, p, h * per : (h + 1) * per
                ]

    prior = prior_buf[0]
    for b in range(batches):
        spread, gain = innovation(prior, value_ref[b : b + 1], err_ref[b : b + 1])
        s_op[b] = spread_operand(spread)
        ghi, glo = split(gain)
        g_op[b] = jnp.concatenate([ghi, glo], axis=0)
        if b + 1 < batches:
            prior = prior_buf[b + 1]
            dlat = (rowl_ref[b + 1 : b + 2] - rowk_ref[b]).astype(jnp.float32)
            dlat = dlat * (1.0 / (2.0 * rows))
            taper = taper_of(dlat * dlat + lon_sq(coll_ref[b + 1 : b + 2] - colk_ref[b]))
            cov = dot(s_op[b], anomaly_operand(prior))
            prior = prior + apply_gain(g_op[b], ghi, taper * cov)

    def assimilate(i0):
        every = [(i0 + j, f) for j in range(ROWS) for f in range(fields)]
        x = [x_ref[i, f] for i, f in every]
        for b in range(batches):
            operand = jnp.concatenate([anomaly_operand(v) for v in x], axis=1)
            cov = dot(s_op[b], operand)
            weighted = jnp.concatenate(
                [
                    taper_buf[b, i] * cov[:, n * cols : (n + 1) * cols]
                    for n, (i, _) in enumerate(every)
                ],
                axis=1,
            )
            change = apply_gain(g_op[b], g_op[b, :members], weighted)
            x = [v + change[:, n * cols : (n + 1) * cols] for n, v in enumerate(x)]
        for (i, f), v in zip(every, x):
            state[0, WIDTH + i, f * members : (f + 1) * members] = v

    def field_slice(c):
        return pl.ds(c * members, members)

    def lat_copy(section, c, down):
        src = rows if down else WIDTH
        dst = 0 if down else WIDTH + rows
        return pltpu.make_async_remote_copy(
            src_ref=state.at[section, pl.ds(src, WIDTH), field_slice(c)],
            dst_ref=state.at[section, pl.ds(dst, WIDTH), field_slice(c)],
            send_sem=lat_send.at[section, c, int(down)],
            recv_sem=lat_recv.at[section, c, int(down)],
            device_id=(lon, lat + 1 if down else lat - 1, lev),
            device_id_type=MESH,
        )

    def lat_start(section, c):
        @pl.when(has_up)
        def _():
            lat_copy(section, c, False).start()

        @pl.when(has_down)
        def _():
            lat_copy(section, c, True).start()

    def lon_copy(section, c, to_east):
        return pltpu.make_async_remote_copy(
            src_ref=packed.at[section, field_slice(c)],
            dst_ref=(left_in if to_east else right_in).at[section, field_slice(c)],
            send_sem=lon_send.at[section, c, int(to_east)],
            recv_sem=lon_recv.at[section, c, int(to_east)],
            device_id=(east if to_east else west, lat, lev),
            device_id_type=MESH,
        )

    per_field = members // SUB

    def lon_start(section, c):
        def step(g, carry):
            sl = pl.ds(pl.multiple_of(c * members + g * SUB, SUB), SUB)
            acc = jnp.zeros((SUB, cols), jnp.float32)
            for r in range(rows):
                rolled = pltpu.roll(state[section, WIDTH + r, sl], WIDTH + slot * r, 1)
                keep = (lane >= slot * r) & (lane < slot * (r + 1))
                acc = jnp.where(keep, rolled, acc)
            packed[section, sl] = acc
            return carry

        lax.fori_loop(0, per_field, step, 0, unroll=5)
        lon_copy(section, c, True).start()
        lon_copy(section, c, False).start()

    last = rows - ROWS
    lax.fori_loop(0, 2, lambda n, carry: (assimilate(n * last), carry)[1], 0)
    for c in range(fields):
        lat_start(0, c)
    lax.fori_loop(1, last // ROWS, lambda n, carry: (assimilate(n * ROWS), carry)[1], 0)

    def do_rows(section, c, first, stop):
        scale = (1.0 / 3.0, 0.5, 1.0)[section]

        def do_row(r, carry):
            shift = lax.rem(2 * cols - WIDTH - slot * r, cols)
            w = [coef[r, o] if o != 10 else None for o in range(14)]
            for g in range(per_field):
                sl = pl.ds(c * members + g * SUB, SUB)
                q = state[section, WIDTH + r, sl]
                t = w[3] * q
                u = jnp.where(edge_lane, pltpu.roll(fix[sl], shift, 1), 0.0)
                for o in (1, 2, 3):
                    t = t + w[3 - o] * pltpu.roll(q, o, 1)
                    u = u + w[3 + o] * pltpu.roll(q, cols - o, 1)
                    t = t + w[10 - o] * state[section, WIDTH + r - o, sl]
                    u = u + w[10 + o] * state[section, WIDTH + r + o, sl]
                base = q if section == 0 else state[0, WIDTH + r, sl]
                if section < 2:
                    state[section + 1, WIDTH + r, sl] = base + (t + u) * scale
                else:
                    at = (g * SUB * fields + c) * rows + r
                    out_ref[pl.ds(at, SUB, stride=fields * rows), :] = base + (t + u)
            return carry

        lax.fori_loop(first, stop, do_row, 0)

    for c in range(fields):
        lon_start(0, c)

    for section in range(3):
        for c in range(fields):
            lon_copy(section, c, True).wait_recv()
            lon_copy(section, c, False).wait_recv()

            def fix_step(g, carry):
                sl = pl.ds(pl.multiple_of(c * members + g * SUB, SUB), SUB)
                d = jnp.where(from_left, left_in[section, sl], right_in[section, sl])
                d = d - packed[section, sl]
                t = jnp.zeros((SUB, cols), jnp.float32)
                for o in (1, 2, 3):
                    t = t + edge_coef[0, o - 1] * pltpu.roll(d, o, 1)
                    t = t + edge_coef[1, o - 1] * pltpu.roll(d, cols - o, 1)
                fix[sl] = t
                return carry

            lax.fori_loop(0, per_field, fix_step, 0, unroll=5)
            do_rows(section, c, WIDTH, rows - WIDTH)

            @pl.when(has_up)
            def _():
                lat_copy(section, c, True).wait_recv()

            @pl.when(has_down)
            def _():
                lat_copy(section, c, False).wait_recv()

            do_rows(section, c, 0, WIDTH)
            do_rows(section, c, rows - WIDTH, rows)
            if section < 2:
                lat_start(section + 1, c)
                lon_start(section + 1, c)

    swap_cand().wait_send()
    wait_all(rs_buf, n_lat - 1, share_send.at[1])
    wait_all(z_buf, n_lon - 1, share_send.at[2])
    wait_all(full.at[lev], n_lat - 1, share_send.at[3])
    swap_full().wait_send()
    for section in range(3):
        for c in range(fields):
            lon_copy(section, c, True).wait_send()
            lon_copy(section, c, False).wait_send()

            @pl.when(has_up)
            def _():
                lat_copy(section, c, False).wait_send()

            @pl.when(has_down)
            def _():
                lat_copy(section, c, True).wait_send()


def on_device(ensemble, courant, obs_value, obs_error, owner_device, columns):
    members, fields, _, rows, cols = ensemble.shape
    dims = tuple(lax.axis_size(a) for a in ("lon", "lat", "lev"))
    n_lon, n_lat, n_lev = dims
    batches, count = columns.shape
    lon_index = owner_device // (n_lat * n_lev)
    lat_index = owner_device // n_lev % n_lat
    obs_rows = lat_index[:, None] * rows + columns // cols
    obs_cols = lon_index[:, None] * cols + columns % cols
    me = (lax.axis_index("lon") * n_lat + lax.axis_index("lat")) * n_lev + lax.axis_index("lev")
    local = jnp.where((owner_device == me)[:, None], columns, -1)

    x = ensemble[:, :, 0].transpose(2, 1, 0, 3)
    total = fields * members
    piece = (members // n_lat * count // LANES, LANES)
    f32, bf16 = jnp.float32, jnp.bfloat16
    vmem = pl.BlockSpec(memory_space=pltpu.VMEM)
    dma = pltpu.SemaphoreType.DMA
    out = pl.pallas_call(
        functools.partial(kernel, dims),
        out_shape=jax.ShapeDtypeStruct((members * fields * rows, cols), f32),
        in_specs=[vmem] * 9,
        out_specs=vmem,
        scratch_shapes=[
            pltpu.VMEM((batches, n_lat) + piece, f32),
            pltpu.VMEM((n_lat,) + piece, f32),
            pltpu.VMEM((n_lat,) + piece, f32),
            pltpu.VMEM((n_lat,) + piece, f32),
            pltpu.VMEM((n_lon,) + piece, f32),
            pltpu.VMEM((batches, n_lat) + piece, f32),
            pltpu.VMEM((batches, members, count), f32),
            pltpu.VMEM((batches, count, 256), bf16),
            pltpu.VMEM((batches, 2 * members, count), bf16),
            pltpu.VMEM((batches, count, cols), f32),
            pltpu.VMEM((batches, count, cols), f32),
            pltpu.VMEM((batches, rows, count, cols), f32),
            pltpu.VMEM((3, rows + 2 * WIDTH, total, cols), f32),
            pltpu.VMEM((3, total, cols), f32),
            pltpu.VMEM((3, total, cols), f32),
            pltpu.VMEM((3, total, cols), f32),
            pltpu.VMEM((total, cols), f32),
            pltpu.VMEM((rows, 14, SUB, cols), f32),
            pltpu.VMEM((2, WIDTH, SUB, cols), f32),
            dma((5,)),
            dma((5,)),
            dma((3, fields, 2)),
            dma((3, fields, 2)),
            dma((3, fields, 2)),
            dma((3, fields, 2)),
        ],
        compiler_params=pltpu.CompilerParams(
            has_side_effects=True, collective_id=0, vmem_limit_bytes=VMEM_LIMIT
        ),
        name="filter_and_advect",
    )(
        x, courant[:, 0], obs_value, obs_error, local,
        obs_rows[:, :, None], obs_cols[:, :, None], obs_rows, obs_cols,
    )
    return out.reshape(ensemble.shape)


def solution(mesh):
    return jax.shard_map(
        on_device,
        mesh=mesh,
        in_specs=(
            P(None, None, "lev", "lat", "lon"),
            P(None, "lev", "lat", "lon"),
            P(),
            P(),
            P(),
            P(),
        ),
        out_specs=P(None, None, "lev", "lat", "lon"),
        check_vma=False,
    )
```

```python
import functools

import jax
import jax.numpy as jnp
from jax import lax
from jax.experimental import pallas as pl
from jax.experimental.pallas import tpu as pltpu
from jax.sharding import PartitionSpec as P

MESH = pl.DeviceIdType.MESH
PLUS_WEIGHTS = (-2.0, 15.0, -60.0, 20.0, 30.0, -3.0)
MINUS_WEIGHTS = (3.0, -30.0, -20.0, 60.0, -15.0, 2.0)
VMEM_LIMIT = 60 * 1024 * 1024
WIDTH = 3
SUB = 8
STEP = 11
SUM_SPAN = 16
PACK_SPAN = 16
LANES = 128


def split(x):
    hi = x.astype(jnp.bfloat16)
    lo = (x - hi.astype(jnp.float32)).astype(jnp.bfloat16)
    return hi, lo


def taper_of(r2):
    inv = lax.rsqrt(jnp.maximum(r2, 1e-30))
    r = r2 * inv
    inner = 1.0 + r2 * (-5.0 / 3.0 + r * (0.625 + r * (0.5 - 0.25 * r)))
    outer = (
        4.0
        - (2.0 / 3.0) * inv
        + r * (-5.0 + r * (5.0 / 3.0 + r * (0.625 + r * (-0.5 + r * (1.0 / 12.0)))))
    )
    return jnp.where(r2 <= 1.0, inner, jnp.where(r2 < 4.0, outer, 0.0))


def dot(a, b):
    return jnp.dot(a, b, preferred_element_type=jnp.float32)


def innovation(prior, value, err):
    members = prior.shape[0]
    centre = jnp.sum(prior, axis=0, keepdims=True) * (1.0 / members)
    spread = prior - centre
    variance = jnp.sum(spread * spread, axis=0, keepdims=True) * (1.0 / (members - 1))
    denominator = variance + err
    factor = 1.0 / (1.0 + jnp.sqrt(err / denominator))
    gain = (value - centre - factor * spread) / denominator
    return spread, gain


def spread_operand(spread):
    members, count = spread.shape
    hi, lo = split(spread * (1.0 / (members - 1)))
    pad = jnp.zeros((256 - 3 * members, count), jnp.float32)
    stacked = jnp.concatenate(
        [hi.astype(jnp.float32), lo.astype(jnp.float32), hi.astype(jnp.float32), pad], axis=0
    )
    return stacked.T.astype(jnp.bfloat16)


def anomaly_operand(x):
    members = x.shape[0]
    a = x - jnp.sum(x, axis=0, keepdims=True) * (1.0 / members)
    hi, lo = split(a)
    pad = jnp.zeros((256 - 3 * members, x.shape[1]), jnp.bfloat16)
    return jnp.concatenate([hi, hi, lo, pad], axis=0)


def apply_gain(gain_stack, gain_hi, weighted):
    members = gain_hi.shape[0]
    hi, lo = split(weighted)
    both = dot(gain_stack, hi)
    return both[:members] + both[members:] + dot(gain_hi, lo)


def kernel(
    dims,
    x_ref, cour_ref, value_ref, err_ref, owner_ref, columns_ref, out_ref,
    cand, rs_buf, z_buf, full, prior_buf,
    s_op, g_op, lon_part, row_part, col_part, taper_buf,
    state, packed, left_in, right_in, lhs, dpm, coef, stencil, picker, slot_mask,
    load_sem, share_send, share_recv, lat_send, lat_recv, lon_send, lon_recv,
):
    n_lon, n_lat, n_lev = dims
    members, fields, _, rows, cols = x_ref.shape
    batches, count = value_ref.shape
    total = fields * members
    lon = lax.axis_index("lon")
    lat = lax.axis_index("lat")
    lev = lax.axis_index("lev")
    has_up = lat > 0
    has_down = lat < n_lat - 1
    east = lax.rem(lon + 1, n_lon)
    west = lax.rem(lon + n_lon - 1, n_lon)
    other_lev = 1 - lev
    slot = 2 * WIDTH
    per = members // n_lat

    def load_start(f):
        def one(i, carry):
            pltpu.make_async_copy(
                x_ref.at[:, f, 0, i],
                state.at[0, WIDTH + i, pl.ds(f * members, members)],
                load_sem.at[f],
            ).start()
            return carry

        lax.fori_loop(0, rows, one, 0)

    def load_wait(f):
        view = state.at[0, pl.ds(WIDTH, rows), pl.ds(f * members, members)]
        pltpu.make_async_copy(view, view, load_sem.at[f]).wait()

    for f in range(fields):
        load_start(f)

    barrier = pltpu.get_barrier_semaphore()

    def greet_lat(t, carry):
        other = lax.rem(lat + t, n_lat)
        for v in range(2):
            pl.semaphore_signal(
                barrier, inc=1, device_id=(lon, other, (lev, other_lev)[v]), device_id_type=MESH
            )
        return carry

    def greet_lon(t, carry):
        pl.semaphore_signal(
            barrier, inc=1, device_id=(lax.rem(lon + t, n_lon), lat, lev), device_id_type=MESH
        )
        return carry

    pl.semaphore_signal(barrier, inc=1, device_id=(lon, lat, other_lev), device_id_type=MESH)
    lax.fori_loop(1, n_lat, greet_lat, 0)
    lax.fori_loop(1, n_lon, greet_lon, 0)

    lat0 = lat * rows
    lon0 = lon * cols
    n_total = cols * n_lon
    me = (lon * n_lat + lat) * n_lev + lev
    local, obs_row, obs_col = [], [], []
    for b in range(batches):
        owner = owner_ref[b]
        columns = columns_ref[b : b + 1]
        local.append(columns + jnp.where(owner == me, 0, n_total * rows * n_lat))
        obs_row.append(owner // n_lev % n_lat * rows + columns // cols)
        obs_col.append(owner // (n_lat * n_lev) * cols + columns % cols)

    @pl.when(jnp.logical_not(has_up))
    def _():
        for s in range(3):
            state[s, 0:WIDTH] = jnp.zeros((WIDTH, total, cols), jnp.float32)

    @pl.when(jnp.logical_not(has_down))
    def _():
        for s in range(3):
            state[s, rows + WIDTH :] = jnp.zeros((WIDTH, total, cols), jnp.float32)

    load_wait(0)

    picked = None
    for pair in range(rows // 2):
        parts = [state[0, WIDTH + 2 * pair + j, 0:members] for j in range(2)]
        x0 = jnp.concatenate(parts, axis=1)
        hi = x0.astype(jnp.bfloat16)
        rest = x0 - hi.astype(jnp.float32)
        mid, lo = split(rest)
        cell = lax.broadcasted_iota(jnp.int32, (2 * cols, count), 0) + pair * 2 * cols
        hot = [
            jnp.where(cell == local[b], 1.0, 0.0).astype(jnp.bfloat16)
            for b in range(batches)
        ]
        term = dot(jnp.concatenate([hi, mid, lo], axis=0), jnp.concatenate(hot, axis=1))
        picked = term if picked is None else picked + term
    picked = picked[:members] + (picked[members : 2 * members] + picked[2 * members :])
    halves = count // LANES
    for b in range(batches):
        for p in range(n_lat):
            for h in range(halves):
                at = b * count + h * LANES
                cand[b, p, h * per : (h + 1) * per] = picked[p * per : (p + 1) * per, at : at + LANES]

    for f in range(1, fields):
        load_wait(f)
    pl.semaphore_wait(barrier, 2 * n_lat + n_lon - 2)

    def field_slice(c):
        return pl.ds(pl.multiple_of(c * members, 16), members)

    def block(i):
        return pl.ds(pl.multiple_of(i * members, 16), members)

    def lat_copy(section, c, down):
        src = rows if down else WIDTH
        dst = 0 if down else WIDTH + rows
        return pltpu.make_async_remote_copy(
            src_ref=state.at[section, pl.ds(src, WIDTH), field_slice(c)],
            dst_ref=state.at[section, pl.ds(dst, WIDTH), field_slice(c)],
            send_sem=lat_send.at[section, c, int(down)],
            recv_sem=lat_recv.at[section, c, int(down)],
            device_id=(lon, lat + 1 if down else lat - 1, lev),
            device_id_type=MESH,
        )

    def lat_start(section, c):
        @pl.when(has_up)
        def _():
            lat_copy(section, c, False).start()

        @pl.when(has_down)
        def _():
            lat_copy(section, c, True).start()

    def lat_wait(section, c):
        @pl.when(has_up)
        def _():
            lat_copy(section, c, True).wait_recv()

        @pl.when(has_down)
        def _():
            lat_copy(section, c, False).wait_recv()

    def lat_sent(section, c):
        @pl.when(has_up)
        def _():
            lat_copy(section, c, False).wait_send()

        @pl.when(has_down)
        def _():
            lat_copy(section, c, True).wait_send()

    def lon_copy(section, c, to_east):
        return pltpu.make_async_remote_copy(
            src_ref=packed.at[section, field_slice(c)],
            dst_ref=(left_in if to_east else right_in).at[section, field_slice(c)],
            send_sem=lon_send.at[section, c, int(to_east)],
            recv_sem=lon_recv.at[section, c, int(to_east)],
            device_id=(east if to_east else west, lat, lev),
            device_id_type=MESH,
        )

    def wait_all(buf, number, sem):
        view = buf.at[pl.ds(0, number)]
        pltpu.make_async_copy(view, view, sem).wait()

    def piece(other, to_lev, sem):
        pltpu.make_async_remote_copy(
            src_ref=cand.at[to_lev, other], dst_ref=rs_buf.at[lev, lat],
            send_sem=share_send.at[sem], recv_sem=share_recv.at[sem],
            device_id=(lon, other, to_lev), device_id_type=MESH,
        ).start()

    def send_piece(t, carry):
        other = lax.rem(lat + t, n_lat)
        piece(other, lev, 1)
        piece(other, other_lev, 0)
        return carry

    def send_sum(t, carry):
        pltpu.make_async_remote_copy(
            src_ref=z_buf.at[lon], dst_ref=z_buf.at[lon],
            send_sem=share_send.at[2], recv_sem=share_recv.at[2],
            device_id=(lax.rem(lon + t, n_lon), lat, lev), device_id_type=MESH,
        ).start()
        return carry

    def result(other, to_lev, sem):
        pltpu.make_async_remote_copy(
            src_ref=full.at[lev, lat], dst_ref=full.at[lev, lat],
            send_sem=share_send.at[sem], recv_sem=share_recv.at[sem],
            device_id=(lon, other, to_lev), device_id_type=MESH,
        ).start()

    def send_total(t, carry):
        other = lax.rem(lat + t, n_lat)
        result(other, lev, 3)
        result(other, other_lev, 4)
        return carry

    def lon_sq(gap):
        gap = jnp.abs(gap)
        gap = jnp.minimum(gap, n_total - gap) * (1.0 / (n_total // 2))
        return gap * gap

    wide = rows + 2 * WIDTH

    def tapers(first, last):
        def one(n, carry):
            b = n // wide
            i = lax.rem(n, wide)
            here = (lat0 + i - WIDTH).astype(jnp.float32)
            for at in range(0, count, 64):
                sl = pl.ds(at, 64)
                dlat = (here - row_part[b, sl]) * (1.0 / (2.0 * rows))
                taper_buf[b, i, sl] = taper_of(dlat * dlat + lon_part[b, sl])
            return carry

        lax.fori_loop(first, last, one, 0)

    piece(lat, other_lev, 0)
    lax.fori_loop(1, n_lat, send_piece, 0)
    lat_start(0, 0)
    rs_buf[lev, lat] = cand[lev, lat]
    for b in range(batches):
        grid_cols = (lon0 + lax.broadcasted_iota(jnp.int32, (count, cols), 1)).astype(jnp.float32)
        wide_col = jnp.broadcast_to(obs_col[b].astype(jnp.float32), (cols, count)).T
        col_part[b] = wide_col
        lon_part[b] = lon_sq(grid_cols - wide_col)
        row_part[b] = jnp.broadcast_to(obs_row[b].astype(jnp.float32), (cols, count)).T
    tapers(0, 16)
    wait_all(rs_buf.at[lev], n_lat - 1, share_recv.at[1])
    wait_all(rs_buf.at[other_lev], n_lat, share_recv.at[0])
    z_buf[lon] = jnp.sum(rs_buf[0], axis=0) + jnp.sum(rs_buf[1], axis=0)
    lax.fori_loop(1, n_lon, send_sum, 0)
    lat_start(0, 1)
    tapers(16, 28)
    wait_all(z_buf, n_lon - 1, share_recv.at[2])
    full[lev, lat] = jnp.sum(z_buf[...], axis=0)
    result(lat, other_lev, 4)
    lax.fori_loop(1, n_lat, send_total, 0)
    lat_start(0, 2)
    tapers(28, 2 * wide)

    for r in range(rows):
        for d in range(2):
            c = jnp.broadcast_to(cour_ref[d, r : r + 1], (SUB, cols))
            up = jnp.maximum(c, 0.0) * (-1.0 / 60.0)
            dn = jnp.minimum(c, 0.0) * (-1.0 / 60.0)
            if d == 0:
                coef[r, 0] = up
                coef[r, 1] = dn
            else:
                for o in range(7):
                    w = PLUS_WEIGHTS[o] * up if o < 6 else jnp.zeros_like(c)
                    if o > 0:
                        w = w + MINUS_WEIGHTS[o - 1] * dn
                    coef[r, 2 + o] = w

    k = lax.broadcasted_iota(jnp.int32, (4 * cols, cols), 0)
    j = lax.broadcasted_iota(jnp.int32, (4 * cols, cols), 1)
    kk = lax.rem(k, cols)
    side = lax.rem(kk, slot)
    halo_col = jnp.where(side < WIDTH, side - WIDTH, cols + side - WIDTH)
    gap = jnp.where(k < 2 * cols, kk, halo_col) - j
    for first, weights, lane0 in ((-3, PLUS_WEIGHTS, 0), (-2, MINUS_WEIGHTS, cols)):
        w = jnp.zeros((4 * cols, cols), jnp.float32)
        for n in range(6):
            w = jnp.where(gap == first + n, weights[n], w)
        stencil[:, lane0 : lane0 + cols] = w.astype(jnp.bfloat16)
    side = lax.rem(j, slot)[: 2 * cols]
    wanted = jnp.where(side < WIDTH, cols - WIDTH + side, side - WIDTH)
    hit = (wanted == kk[: 2 * cols]) & (j[: 2 * cols] < slot * rows)
    picker[...] = jnp.where(hit, 1.0, 0.0).astype(jnp.bfloat16)

    lane = lax.broadcasted_iota(jnp.int32, (members, cols), 1)
    from_left = lax.rem(lane, slot) < WIDTH
    slot_of = lane // slot
    for r in range(rows):
        slot_mask[r] = jnp.where(slot_of == r, 1.0, 0.0).astype(jnp.bfloat16)

    wait_all(full.at[lev], n_lat - 1, share_recv.at[3])
    wait_all(full.at[other_lev], n_lat, share_recv.at[4])
    for b in range(batches):
        for p in range(n_lat):
            for h in range(halves):
                at = h * LANES
                prior_buf[b, p * per : (p + 1) * per, at : at + LANES] = full[
                    b, p, h * per : (h + 1) * per
                ]

    prior = prior_buf[0]
    for b in range(batches):
        spread, gain = innovation(prior, value_ref[b : b + 1], err_ref[b : b + 1])
        s_op[b] = spread_operand(spread)
        ghi, glo = split(gain)
        g_op[b] = jnp.concatenate([ghi, glo], axis=0)
        if b + 1 < batches:
            prior = prior_buf[b + 1]
            both = [jnp.concatenate([v[b]] * halves, axis=1) for v in (row_part, col_part)]
            dlat = (obs_row[b + 1].astype(jnp.float32) - both[0]) * (1.0 / (2.0 * rows))
            taper = taper_of(dlat * dlat + lon_sq(obs_col[b + 1].astype(jnp.float32) - both[1]))
            cov = dot(s_op[b], anomaly_operand(prior))
            prior = prior + apply_gain(g_op[b], ghi, taper * cov)

    def assimilate(c):
        def step(n, carry):
            at = [n * STEP + j for j in range(STEP)]
            x = [state[0, i, field_slice(c)] for i in at]
            for b in range(batches):
                operand = jnp.concatenate([anomaly_operand(v) for v in x], axis=1)
                cov = dot(s_op[b], operand)
                weighted = jnp.concatenate(
                    [
                        taper_buf[b, i] * cov[:, j * cols : (j + 1) * cols]
                        for j, i in enumerate(at)
                    ],
                    axis=1,
                )
                change = apply_gain(g_op[b], g_op[b, :members], weighted)
                x = [v + change[:, j * cols : (j + 1) * cols] for j, v in enumerate(x)]
            for i, v in zip(at, x):
                state[0, i, field_slice(c)] = v
                hi, lo = split(v)
                lhs[c, block(i), 0:cols] = hi
                lhs[c, block(i), cols : 2 * cols] = lo
            return carry

        lax.fori_loop(0, wide // STEP, step, 0)


    def lon_start(section, c):
        def step(n, acc):
            at = pl.multiple_of((WIDTH + n * PACK_SPAN) * members, 16)
            got = dot(lhs[c, pl.ds(at, PACK_SPAN * members), 0 : 2 * cols], picker[...])
            for m in range(PACK_SPAN):
                acc = jnp.where(slot_of == n * PACK_SPAN + m, got[m * members : (m + 1) * members], acc)
            return acc

        zero = jnp.zeros((members, cols), jnp.float32)
        packed[section, field_slice(c)] = lax.fori_loop(0, rows // PACK_SPAN, step, zero)
        lon_copy(section, c, True).start()
        lon_copy(section, c, False).start()

    def lon_finish(section, c):
        lon_copy(section, c, True).wait_recv()
        lon_copy(section, c, False).wait_recv()
        halo = jnp.where(
            from_left, left_in[section, field_slice(c)], right_in[section, field_slice(c)]
        )

        parts = split(halo)

        def step(n, carry):
            for m in range(SUM_SPAN):
                r = n * SUM_SPAN + m
                for p in range(2):
                    lanes = slice((2 + p) * cols, (3 + p) * cols)
                    lhs[c, block(WIDTH + r), lanes] = parts[p] * slot_mask[r]
            at = pl.multiple_of((WIDTH + n * SUM_SPAN) * members, 16)
            to = pl.multiple_of(n * SUM_SPAN * members, 16)
            rows_in = pl.ds(at, SUM_SPAN * members)
            dpm[pl.ds(to, SUM_SPAN * members)] = dot(lhs[c, rows_in], stencil[...])
            return carry

        lax.fori_loop(0, rows // SUM_SPAN, step, 0)

    def do_rows(section, c, first, stop):
        scale = (1.0 / 3.0, 0.5, 1.0)[section]

        def do_row(n, carry):
            r = n if isinstance(first, int) else first(n)
            w = [jnp.concatenate([coef[r, o]] * 2, axis=0) for o in range(9)]
            for g in range(members // (2 * SUB)):
                off = g * 2 * SUB
                sl = pl.ds(pl.multiple_of(c * members + off, 2 * SUB), 2 * SUB)
                at = pl.ds(pl.multiple_of(r * members + off, 2 * SUB), 2 * SUB)
                q = state[section, WIDTH + r, sl]
                t = w[0] * dpm[at, 0:cols]
                u = w[1] * dpm[at, cols : 2 * cols] + w[5] * q
                for o in (1, 2, 3):
                    t = t + w[5 - o] * state[section, WIDTH + r - o, sl]
                    u = u + w[5 + o] * state[section, WIDTH + r + o, sl]
                base = q if section == 0 else state[0, WIDTH + r, sl]
                if section < 2:
                    value = base + (t + u) * scale
                    state[section + 1, WIDTH + r, sl] = value
                    hi, lo = split(value)
                    to = pl.ds(pl.multiple_of((WIDTH + r) * members + off, 2 * SUB), 2 * SUB)
                    lhs[c, to, 0:cols] = hi
                    lhs[c, to, cols : 2 * cols] = lo
                else:
                    at = (off * fields + c) * rows + r
                    out_ref[pl.ds(at, 2 * SUB, stride=fields * rows), :] = base + (t + u)
            return carry

        lax.fori_loop(first if isinstance(first, int) else 0, stop, do_row, 0)

    def interior(section, c):
        do_rows(section, c, WIDTH, rows - WIDTH)

    def edges(section, c):
        def edge_row(n):
            return jnp.where(n < WIDTH, n, n + rows - 2 * WIDTH)

        do_rows(section, c, edge_row, 2 * WIDTH)

    def first_pass(c, carry):
        @pl.when(c < fields)
        def _():
            lat_wait(0, c)
            lat_sent(0, c)
            assimilate(c)
            lon_start(0, c)

        @pl.when(c > 0)
        def _():
            lon_finish(0, c - 1)
            edges(0, c - 1)
            lat_start(1, c - 1)
            interior(0, c - 1)
            lon_start(1, c - 1)

        return carry

    lax.fori_loop(0, fields + 1, first_pass, 0)

    for section in (1, 2):

        def later_pass(c, carry):
            lon_finish(section, c)
            interior(section, c)
            lat_wait(section, c)
            edges(section, c)
            if section < 2:
                lat_start(section + 1, c)
                lon_start(section + 1, c)
            return carry

        lax.fori_loop(0, fields, later_pass, 0)

    wait_all(rs_buf.at[lev], n_lat - 1, share_send.at[1])
    wait_all(rs_buf.at[other_lev], n_lat, share_send.at[0])
    wait_all(z_buf, n_lon - 1, share_send.at[2])
    wait_all(full.at[lev], n_lat - 1, share_send.at[3])
    wait_all(full.at[other_lev], n_lat, share_send.at[4])
    for section in range(3):
        for c in range(fields):
            lon_copy(section, c, True).wait_send()
            lon_copy(section, c, False).wait_send()
            if section > 0:
                lat_sent(section, c)


def on_device(ensemble, courant, obs_value, obs_error, owner_device, columns):
    members, fields, _, rows, cols = ensemble.shape
    dims = tuple(lax.axis_size(a) for a in ("lon", "lat", "lev"))
    n_lon, n_lat, _ = dims
    batches, count = columns.shape
    total = fields * members
    piece = (members // n_lat * count // LANES, LANES)
    f32, bf16 = jnp.float32, jnp.bfloat16
    vmem = pl.BlockSpec(memory_space=pltpu.VMEM)
    smem = pl.BlockSpec(memory_space=pltpu.SMEM)
    dma = pltpu.SemaphoreType.DMA
    out = pl.pallas_call(
        functools.partial(kernel, dims),
        out_shape=jax.ShapeDtypeStruct((members * fields * rows, cols), f32),
        in_specs=[pl.BlockSpec(memory_space=pl.ANY)] + [vmem] * 3 + [smem, vmem],
        out_specs=vmem,
        scratch_shapes=[
            pltpu.VMEM((batches, n_lat) + piece, f32),
            pltpu.VMEM((batches, n_lat) + piece, f32),
            pltpu.VMEM((n_lon,) + piece, f32),
            pltpu.VMEM((batches, n_lat) + piece, f32),
            pltpu.VMEM((batches, members, count), f32),
            pltpu.VMEM((batches, count, 256), bf16),
            pltpu.VMEM((batches, 2 * members, count), bf16),
            pltpu.VMEM((batches, count, cols), f32),
            pltpu.VMEM((batches, count, cols), f32),
            pltpu.VMEM((batches, count, cols), f32),
            pltpu.VMEM((batches, rows + 2 * WIDTH, count, cols), f32),
            pltpu.VMEM((3, rows + 2 * WIDTH, total, cols), f32),
            pltpu.VMEM((3, total, cols), f32),
            pltpu.VMEM((3, total, cols), f32),
            pltpu.VMEM((3, total, cols), f32),
            pltpu.VMEM((fields, (rows + 2 * WIDTH) * members, 4 * cols), bf16),
            pltpu.VMEM((rows * members, 2 * cols), f32),
            pltpu.VMEM((rows, 9, SUB, cols), f32),
            pltpu.VMEM((4 * cols, 2 * cols), bf16),
            pltpu.VMEM((2 * cols, cols), bf16),
            pltpu.VMEM((rows, members, cols), bf16),
            dma((fields,)),
            dma((5,)),
            dma((5,)),
            dma((3, fields, 2)),
            dma((3, fields, 2)),
            dma((3, fields, 2)),
            dma((3, fields, 2)),
        ],
        compiler_params=pltpu.CompilerParams(
            has_side_effects=True, collective_id=0, vmem_limit_bytes=VMEM_LIMIT
        ),
        name="filter_and_advect",
    )(
        ensemble, courant[:, 0], obs_value, obs_error, owner_device, columns,
    )
    return out.reshape(ensemble.shape)


def solution(mesh):
    return jax.shard_map(
        on_device,
        mesh=mesh,
        in_specs=(
            P(None, None, "lev", "lat", "lon"),
            P(None, "lev", "lat", "lon"),
            P(),
            P(),
            P(),
            P(),
        ),
        out_specs=P(None, None, "lev", "lat", "lon"),
        check_vma=False,
    )
```

```python
import functools

import jax
import jax.numpy as jnp
from jax import lax
from jax.experimental import pallas as pl
from jax.experimental.pallas import tpu as pltpu
from jax.sharding import PartitionSpec as P

MESH = pl.DeviceIdType.MESH
PLUS_WEIGHTS = (-2.0, 15.0, -60.0, 20.0, 30.0, -3.0)
MINUS_WEIGHTS = (3.0, -30.0, -20.0, 60.0, -15.0, 2.0)
VMEM_LIMIT = 60 * 1024 * 1024
WIDTH = 3
SUB = 8
STEP = 22
SUM_SPAN = 16
PACK_SPAN = 16
LANES = 128


def split(x):
    hi = x.astype(jnp.bfloat16)
    lo = (x - hi.astype(jnp.float32)).astype(jnp.bfloat16)
    return hi, lo


def taper_of(r2):
    inv = lax.rsqrt(jnp.maximum(r2, 1e-30))
    r = r2 * inv
    inner = 1.0 + r2 * (-5.0 / 3.0 + r * (0.625 + r * (0.5 - 0.25 * r)))
    outer = (
        4.0
        - (2.0 / 3.0) * inv
        + r * (-5.0 + r * (5.0 / 3.0 + r * (0.625 + r * (-0.5 + r * (1.0 / 12.0)))))
    )
    return jnp.where(r2 <= 1.0, inner, jnp.where(r2 < 4.0, outer, 0.0))


def dot(a, b):
    return jnp.dot(a, b, preferred_element_type=jnp.float32)


def innovation(prior, value, err):
    members = prior.shape[0]
    centre = jnp.sum(prior, axis=0, keepdims=True) * (1.0 / members)
    spread = prior - centre
    variance = jnp.sum(spread * spread, axis=0, keepdims=True) * (1.0 / (members - 1))
    denominator = variance + err
    factor = 1.0 / (1.0 + jnp.sqrt(err / denominator))
    gain = (value - centre - factor * spread) / denominator
    return spread, gain


def spread_operand(spread):
    members, count = spread.shape
    hi, lo = split(spread * (1.0 / (members - 1)))
    pad = jnp.zeros((256 - 3 * members, count), jnp.float32)
    stacked = jnp.concatenate(
        [hi.astype(jnp.float32), lo.astype(jnp.float32), hi.astype(jnp.float32), pad], axis=0
    )
    return stacked.T.astype(jnp.bfloat16)


def anomaly_operand(x):
    members = x.shape[0]
    a = x - jnp.sum(x, axis=0, keepdims=True) * (1.0 / members)
    hi, lo = split(a)
    pad = jnp.zeros((256 - 3 * members, x.shape[1]), jnp.bfloat16)
    return jnp.concatenate([hi, hi, lo, pad], axis=0)


def apply_gain(gain_stack, gain_hi, weighted):
    members = gain_hi.shape[0]
    hi, lo = split(weighted)
    both = dot(gain_stack, hi)
    return both[:members] + both[members:] + dot(gain_hi, lo)


def kernel(
    dims,
    x_ref, cour_ref, value_ref, err_ref, owner_ref, columns_ref, out_ref,
    cand, rs_buf, z_buf, full, prior_buf,
    s_op, g_op, lon_part, row_part, col_part, taper_buf,
    state, packed, left_in, right_in, lhs, dpm, coef, stencil, picker, slot_mask,
    load_sem, share_send, share_recv, lat_send, lat_recv, lon_send, lon_recv,
):
    n_lon, n_lat, n_lev = dims
    members, fields, _, rows, cols = x_ref.shape
    batches, count = value_ref.shape
    total = fields * members
    lon = lax.axis_index("lon")
    lat = lax.axis_index("lat")
    lev = lax.axis_index("lev")
    has_up = lat > 0
    has_down = lat < n_lat - 1
    east = lax.rem(lon + 1, n_lon)
    west = lax.rem(lon + n_lon - 1, n_lon)
    other_lev = 1 - lev
    slot = 2 * WIDTH
    per = members // n_lat

    def load_start(f):
        def one(i, carry):
            pltpu.make_async_copy(
                x_ref.at[:, f, 0, i],
                state.at[0, WIDTH + i, pl.ds(f * members, members)],
                load_sem.at[f],
            ).start()
            return carry

        lax.fori_loop(0, rows, one, 0)

    def load_wait(f):
        view = state.at[0, pl.ds(WIDTH, rows), pl.ds(f * members, members)]
        pltpu.make_async_copy(view, view, load_sem.at[f]).wait()

    for f in range(fields):
        load_start(f)

    barrier = pltpu.get_barrier_semaphore()

    def greet_lat(t, carry):
        other = lax.rem(lat + t, n_lat)
        for v in range(2):
            pl.semaphore_signal(
                barrier, inc=1, device_id=(lon, other, (lev, other_lev)[v]), device_id_type=MESH
            )
        return carry

    def greet_lon(t, carry):
        pl.semaphore_signal(
            barrier, inc=1, device_id=(lax.rem(lon + t, n_lon), lat, lev), device_id_type=MESH
        )
        return carry

    pl.semaphore_signal(barrier, inc=1, device_id=(lon, lat, other_lev), device_id_type=MESH)
    lax.fori_loop(1, n_lat, greet_lat, 0)
    lax.fori_loop(1, n_lon, greet_lon, 0)

    lat0 = lat * rows
    lon0 = lon * cols
    n_total = cols * n_lon
    me = (lon * n_lat + lat) * n_lev + lev
    local, obs_row, obs_col = [], [], []
    for b in range(batches):
        owner = owner_ref[b]
        columns = columns_ref[b : b + 1]
        local.append(columns + jnp.where(owner == me, 0, n_total * rows * n_lat))
        obs_row.append(owner // n_lev % n_lat * rows + columns // cols)
        obs_col.append(owner // (n_lat * n_lev) * cols + columns % cols)

    @pl.when(jnp.logical_not(has_up))
    def _():
        for s in range(3):
            state[s, 0:WIDTH] = jnp.zeros((WIDTH, total, cols), jnp.float32)

    @pl.when(jnp.logical_not(has_down))
    def _():
        for s in range(3):
            state[s, rows + WIDTH :] = jnp.zeros((WIDTH, total, cols), jnp.float32)

    load_wait(0)

    picked = None
    for pair in range(rows // 2):
        parts = [state[0, WIDTH + 2 * pair + j, 0:members] for j in range(2)]
        x0 = jnp.concatenate(parts, axis=1)
        hi = x0.astype(jnp.bfloat16)
        rest = x0 - hi.astype(jnp.float32)
        mid, lo = split(rest)
        cell = lax.broadcasted_iota(jnp.int32, (2 * cols, count), 0) + pair * 2 * cols
        hot = [
            jnp.where(cell == local[b], 1.0, 0.0).astype(jnp.bfloat16)
            for b in range(batches)
        ]
        term = dot(jnp.concatenate([hi, mid, lo], axis=0), jnp.concatenate(hot, axis=1))
        picked = term if picked is None else picked + term
    picked = picked[:members] + (picked[members : 2 * members] + picked[2 * members :])
    halves = count // LANES
    for b in range(batches):
        for p in range(n_lat):
            for h in range(halves):
                at = b * count + h * LANES
                cand[b, p, h * per : (h + 1) * per] = picked[p * per : (p + 1) * per, at : at + LANES]

    for f in range(1, fields):
        load_wait(f)
    pl.semaphore_wait(barrier, 2 * n_lat + n_lon - 2)

    def field_slice(c):
        return pl.ds(pl.multiple_of(c * members, 16), members)

    def block(i):
        return pl.ds(pl.multiple_of(i * members, 16), members)

    def lat_copy(section, c, down):
        src = rows if down else WIDTH
        dst = 0 if down else WIDTH + rows
        return pltpu.make_async_remote_copy(
            src_ref=state.at[section, pl.ds(src, WIDTH), field_slice(c)],
            dst_ref=state.at[section, pl.ds(dst, WIDTH), field_slice(c)],
            send_sem=lat_send.at[section, c, int(down)],
            recv_sem=lat_recv.at[section, c, int(down)],
            device_id=(lon, lat + 1 if down else lat - 1, lev),
            device_id_type=MESH,
        )

    def lat_start(section, c):
        @pl.when(has_up)
        def _():
            lat_copy(section, c, False).start()

        @pl.when(has_down)
        def _():
            lat_copy(section, c, True).start()

    def lat_wait(section, c):
        @pl.when(has_up)
        def _():
            lat_copy(section, c, True).wait_recv()

        @pl.when(has_down)
        def _():
            lat_copy(section, c, False).wait_recv()

    def lat_sent(section, c):
        @pl.when(has_up)
        def _():
            lat_copy(section, c, False).wait_send()

        @pl.when(has_down)
        def _():
            lat_copy(section, c, True).wait_send()

    def lon_copy(section, c, to_east):
        return pltpu.make_async_remote_copy(
            src_ref=packed.at[section, field_slice(c)],
            dst_ref=(left_in if to_east else right_in).at[section, field_slice(c)],
            send_sem=lon_send.at[section, c, int(to_east)],
            recv_sem=lon_recv.at[section, c, int(to_east)],
            device_id=(east if to_east else west, lat, lev),
            device_id_type=MESH,
        )

    def wait_all(buf, number, sem):
        view = buf.at[pl.ds(0, number)]
        pltpu.make_async_copy(view, view, sem).wait()

    def piece(other, to_lev, sem):
        pltpu.make_async_remote_copy(
            src_ref=cand.at[to_lev, other], dst_ref=rs_buf.at[lev, lat],
            send_sem=share_send.at[sem], recv_sem=share_recv.at[sem],
            device_id=(lon, other, to_lev), device_id_type=MESH,
        ).start()

    def send_piece(t, carry):
        other = lax.rem(lat + t, n_lat)
        piece(other, lev, 1)
        piece(other, other_lev, 0)
        return carry

    def send_sum(t, carry):
        pltpu.make_async_remote_copy(
            src_ref=z_buf.at[lon], dst_ref=z_buf.at[lon],
            send_sem=share_send.at[2], recv_sem=share_recv.at[2],
            device_id=(lax.rem(lon + t, n_lon), lat, lev), device_id_type=MESH,
        ).start()
        return carry

    def result(other, to_lev, sem):
        pltpu.make_async_remote_copy(
            src_ref=full.at[lev, lat], dst_ref=full.at[lev, lat],
            send_sem=share_send.at[sem], recv_sem=share_recv.at[sem],
            device_id=(lon, other, to_lev), device_id_type=MESH,
        ).start()

    def send_total(t, carry):
        other = lax.rem(lat + t, n_lat)
        result(other, lev, 3)
        result(other, other_lev, 4)
        return carry

    def lon_sq(gap):
        gap = jnp.abs(gap)
        gap = jnp.minimum(gap, n_total - gap) * (1.0 / (n_total // 2))
        return gap * gap

    wide = rows + 2 * WIDTH

    def tapers(first, last):
        def one(n, carry):
            b = n // wide
            i = lax.rem(n, wide)
            here = (lat0 + i - WIDTH).astype(jnp.float32)
            for at in range(0, count, 64):
                sl = pl.ds(at, 64)
                dlat = (here - row_part[b, sl]) * (1.0 / (2.0 * rows))
                taper_buf[b, i, sl] = taper_of(dlat * dlat + lon_part[b, sl])
            return carry

        lax.fori_loop(first, last, one, 0)

    piece(lat, other_lev, 0)
    lax.fori_loop(1, n_lat, send_piece, 0)
    lat_start(0, 0)
    rs_buf[lev, lat] = cand[lev, lat]
    for b in range(batches):
        grid_cols = (lon0 + lax.broadcasted_iota(jnp.int32, (count, cols), 1)).astype(jnp.float32)
        wide_col = jnp.broadcast_to(obs_col[b].astype(jnp.float32), (cols, count)).T
        col_part[b] = wide_col
        lon_part[b] = lon_sq(grid_cols - wide_col)
        row_part[b] = jnp.broadcast_to(obs_row[b].astype(jnp.float32), (cols, count)).T
    tapers(0, 16)
    wait_all(rs_buf.at[lev], n_lat - 1, share_recv.at[1])
    wait_all(rs_buf.at[other_lev], n_lat, share_recv.at[0])
    z_buf[lon] = jnp.sum(rs_buf[0], axis=0) + jnp.sum(rs_buf[1], axis=0)
    lax.fori_loop(1, n_lon, send_sum, 0)
    lat_start(0, 1)
    tapers(16, 28)
    wait_all(z_buf, n_lon - 1, share_recv.at[2])
    full[lev, lat] = jnp.sum(z_buf[...], axis=0)
    result(lat, other_lev, 4)
    lax.fori_loop(1, n_lat, send_total, 0)
    lat_start(0, 2)
    tapers(28, 2 * wide)

    for r in range(rows):
        for d in range(2):
            c = jnp.broadcast_to(cour_ref[d, r : r + 1], (SUB, cols))
            up = jnp.maximum(c, 0.0) * (-1.0 / 60.0)
            dn = jnp.minimum(c, 0.0) * (-1.0 / 60.0)
            if d == 0:
                coef[r, 0] = up
                coef[r, 1] = dn
            else:
                for o in range(7):
                    w = PLUS_WEIGHTS[o] * up if o < 6 else jnp.zeros_like(c)
                    if o > 0:
                        w = w + MINUS_WEIGHTS[o - 1] * dn
                    coef[r, 2 + o] = w

    k = lax.broadcasted_iota(jnp.int32, (4 * cols, cols), 0)
    j = lax.broadcasted_iota(jnp.int32, (4 * cols, cols), 1)
    kk = lax.rem(k, cols)
    side = lax.rem(kk, slot)
    halo_col = jnp.where(side < WIDTH, side - WIDTH, cols + side - WIDTH)
    gap = jnp.where(k < 2 * cols, kk, halo_col) - j
    for first, weights, lane0 in ((-3, PLUS_WEIGHTS, 0), (-2, MINUS_WEIGHTS, cols)):
        w = jnp.zeros((4 * cols, cols), jnp.float32)
        for n in range(6):
            w = jnp.where(gap == first + n, weights[n], w)
        stencil[:, lane0 : lane0 + cols] = w.astype(jnp.bfloat16)
    side = lax.rem(j, slot)[: 2 * cols]
    wanted = jnp.where(side < WIDTH, cols - WIDTH + side, side - WIDTH)
    hit = (wanted == kk[: 2 * cols]) & (j[: 2 * cols] < slot * rows)
    picker[...] = jnp.where(hit, 1.0, 0.0).astype(jnp.bfloat16)

    lane = lax.broadcasted_iota(jnp.int32, (members, cols), 1)
    from_left = lax.rem(lane, slot) < WIDTH
    slot_of = lane // slot
    for r in range(rows):
        slot_mask[r] = jnp.where(slot_of == r, 1.0, 0.0).astype(jnp.bfloat16)

    wait_all(full.at[lev], n_lat - 1, share_recv.at[3])
    wait_all(full.at[other_lev], n_lat, share_recv.at[4])
    for b in range(batches):
        for p in range(n_lat):
            for h in range(halves):
                at = h * LANES
                prior_buf[b, p * per : (p + 1) * per, at : at + LANES] = full[
                    b, p, h * per : (h + 1) * per
                ]

    prior = prior_buf[0]
    for b in range(batches):
        spread, gain = innovation(prior, value_ref[b : b + 1], err_ref[b : b + 1])
        s_op[b] = spread_operand(spread)
        ghi, glo = split(gain)
        g_op[b] = jnp.concatenate([ghi, glo], axis=0)
        if b + 1 < batches:
            prior = prior_buf[b + 1]
            both = [jnp.concatenate([v[b]] * halves, axis=1) for v in (row_part, col_part)]
            dlat = (obs_row[b + 1].astype(jnp.float32) - both[0]) * (1.0 / (2.0 * rows))
            taper = taper_of(dlat * dlat + lon_sq(obs_col[b + 1].astype(jnp.float32) - both[1]))
            cov = dot(s_op[b], anomaly_operand(prior))
            prior = prior + apply_gain(g_op[b], ghi, taper * cov)

    def assimilate(c):
        def step(n, carry):
            at = [n * STEP + j for j in range(STEP)]
            x = [state[0, i, field_slice(c)] for i in at]
            for b in range(batches):
                operand = jnp.concatenate([anomaly_operand(v) for v in x], axis=1)
                cov = dot(s_op[b], operand)
                weighted = jnp.concatenate(
                    [
                        taper_buf[b, i] * cov[:, j * cols : (j + 1) * cols]
                        for j, i in enumerate(at)
                    ],
                    axis=1,
                )
                change = apply_gain(g_op[b], g_op[b, :members], weighted)
                x = [v + change[:, j * cols : (j + 1) * cols] for j, v in enumerate(x)]
            for i, v in zip(at, x):
                state[0, i, field_slice(c)] = v
                hi, lo = split(v)
                lhs[c, block(i), 0:cols] = hi
                lhs[c, block(i), cols : 2 * cols] = lo
            return carry

        lax.fori_loop(0, wide // STEP, step, 0)


    def lon_start(section, c):
        def step(n, acc):
            at = pl.multiple_of((WIDTH + n * PACK_SPAN) * members, 16)
            got = dot(lhs[c, pl.ds(at, PACK_SPAN * members), 0 : 2 * cols], picker[...])
            for m in range(PACK_SPAN):
                acc = jnp.where(slot_of == n * PACK_SPAN + m, got[m * members : (m + 1) * members], acc)
            return acc

        zero = jnp.zeros((members, cols), jnp.float32)
        packed[section, field_slice(c)] = lax.fori_loop(0, rows // PACK_SPAN, step, zero)
        lon_copy(section, c, True).start()
        lon_copy(section, c, False).start()

    def lon_finish(section, c):
        lon_copy(section, c, True).wait_recv()
        lon_copy(section, c, False).wait_recv()
        halo = jnp.where(
            from_left, left_in[section, field_slice(c)], right_in[section, field_slice(c)]
        )

        parts = split(halo)

        def step(n, carry):
            for m in range(SUM_SPAN):
                r = n * SUM_SPAN + m
                for p in range(2):
                    lanes = slice((2 + p) * cols, (3 + p) * cols)
                    lhs[c, block(WIDTH + r), lanes] = parts[p] * slot_mask[r]
            at = pl.multiple_of((WIDTH + n * SUM_SPAN) * members, 16)
            to = pl.multiple_of(n * SUM_SPAN * members, 16)
            rows_in = pl.ds(at, SUM_SPAN * members)
            dpm[pl.ds(to, SUM_SPAN * members)] = dot(lhs[c, rows_in], stencil[...])
            return carry

        lax.fori_loop(0, rows // SUM_SPAN, step, 0)

    def do_rows(section, c, first, stop):
        scale = (1.0 / 3.0, 0.5, 1.0)[section]

        def do_row(n, carry):
            r = n if isinstance(first, int) else first(n)
            w = [jnp.concatenate([coef[r, o]] * 2, axis=0) for o in range(9)]
            for g in range(members // (2 * SUB)):
                off = g * 2 * SUB
                sl = pl.ds(pl.multiple_of(c * members + off, 2 * SUB), 2 * SUB)
                at = pl.ds(pl.multiple_of(r * members + off, 2 * SUB), 2 * SUB)
                q = state[section, WIDTH + r, sl]
                t = w[0] * dpm[at, 0:cols]
                u = w[1] * dpm[at, cols : 2 * cols] + w[5] * q
                for o in (1, 2, 3):
                    t = t + w[5 - o] * state[section, WIDTH + r - o, sl]
                    u = u + w[5 + o] * state[section, WIDTH + r + o, sl]
                base = q if section == 0 else state[0, WIDTH + r, sl]
                if section < 2:
                    value = base + (t + u) * scale
                    state[section + 1, WIDTH + r, sl] = value
                    hi, lo = split(value)
                    to = pl.ds(pl.multiple_of((WIDTH + r) * members + off, 2 * SUB), 2 * SUB)
                    lhs[c, to, 0:cols] = hi
                    lhs[c, to, cols : 2 * cols] = lo
                else:
                    at = (off * fields + c) * rows + r
                    out_ref[pl.ds(at, 2 * SUB, stride=fields * rows), :] = base + (t + u)
            return carry

        lax.fori_loop(first if isinstance(first, int) else 0, stop, do_row, 0)

    def interior(section, c):
        do_rows(section, c, WIDTH, rows - WIDTH)

    def edges(section, c):
        def edge_row(n):
            return jnp.where(n < WIDTH, n, n + rows - 2 * WIDTH)

        do_rows(section, c, edge_row, 2 * WIDTH)

    def first_pass(c, carry):
        @pl.when(c < fields)
        def _():
            lat_wait(0, c)
            lat_sent(0, c)
            assimilate(c)
            lon_start(0, c)

        @pl.when(c > 0)
        def _():
            lon_finish(0, c - 1)
            edges(0, c - 1)
            lat_start(1, c - 1)
            interior(0, c - 1)
            lon_start(1, c - 1)

        return carry

    lax.fori_loop(0, fields + 1, first_pass, 0)

    for section in (1, 2):

        def later_pass(c, carry):
            lon_finish(section, c)
            interior(section, c)
            lat_wait(section, c)
            edges(section, c)
            if section < 2:
                lat_start(section + 1, c)
                lon_start(section + 1, c)
            return carry

        lax.fori_loop(0, fields, later_pass, 0)

    wait_all(rs_buf.at[lev], n_lat - 1, share_send.at[1])
    wait_all(rs_buf.at[other_lev], n_lat, share_send.at[0])
    wait_all(z_buf, n_lon - 1, share_send.at[2])
    wait_all(full.at[lev], n_lat - 1, share_send.at[3])
    wait_all(full.at[other_lev], n_lat, share_send.at[4])
    for section in range(3):
        for c in range(fields):
            lon_copy(section, c, True).wait_send()
            lon_copy(section, c, False).wait_send()
            if section > 0:
                lat_sent(section, c)


def on_device(ensemble, courant, obs_value, obs_error, owner_device, columns):
    members, fields, _, rows, cols = ensemble.shape
    dims = tuple(lax.axis_size(a) for a in ("lon", "lat", "lev"))
    n_lon, n_lat, _ = dims
    batches, count = columns.shape
    total = fields * members
    piece = (members // n_lat * count // LANES, LANES)
    f32, bf16 = jnp.float32, jnp.bfloat16
    vmem = pl.BlockSpec(memory_space=pltpu.VMEM)
    smem = pl.BlockSpec(memory_space=pltpu.SMEM)
    dma = pltpu.SemaphoreType.DMA
    out = pl.pallas_call(
        functools.partial(kernel, dims),
        out_shape=jax.ShapeDtypeStruct((members * fields * rows, cols), f32),
        in_specs=[pl.BlockSpec(memory_space=pl.ANY)] + [vmem] * 3 + [smem, vmem],
        out_specs=vmem,
        scratch_shapes=[
            pltpu.VMEM((batches, n_lat) + piece, f32),
            pltpu.VMEM((batches, n_lat) + piece, f32),
            pltpu.VMEM((n_lon,) + piece, f32),
            pltpu.VMEM((batches, n_lat) + piece, f32),
            pltpu.VMEM((batches, members, count), f32),
            pltpu.VMEM((batches, count, 256), bf16),
            pltpu.VMEM((batches, 2 * members, count), bf16),
            pltpu.VMEM((batches, count, cols), f32),
            pltpu.VMEM((batches, count, cols), f32),
            pltpu.VMEM((batches, count, cols), f32),
            pltpu.VMEM((batches, rows + 2 * WIDTH, count, cols), f32),
            pltpu.VMEM((3, rows + 2 * WIDTH, total, cols), f32),
            pltpu.VMEM((3, total, cols), f32),
            pltpu.VMEM((3, total, cols), f32),
            pltpu.VMEM((3, total, cols), f32),
            pltpu.VMEM((fields, (rows + 2 * WIDTH) * members, 4 * cols), bf16),
            pltpu.VMEM((rows * members, 2 * cols), f32),
            pltpu.VMEM((rows, 9, SUB, cols), f32),
            pltpu.VMEM((4 * cols, 2 * cols), bf16),
            pltpu.VMEM((2 * cols, cols), bf16),
            pltpu.VMEM((rows, members, cols), bf16),
            dma((fields,)),
            dma((5,)),
            dma((5,)),
            dma((3, fields, 2)),
            dma((3, fields, 2)),
            dma((3, fields, 2)),
            dma((3, fields, 2)),
        ],
        compiler_params=pltpu.CompilerParams(
            has_side_effects=True, collective_id=0, vmem_limit_bytes=VMEM_LIMIT
        ),
        name="filter_and_advect",
    )(
        ensemble, courant[:, 0], obs_value, obs_error, owner_device, columns,
    )
    return out.reshape(ensemble.shape)


def solution(mesh):
    return jax.shard_map(
        on_device,
        mesh=mesh,
        in_specs=(
            P(None, None, "lev", "lat", "lon"),
            P(None, "lev", "lat", "lon"),
            P(),
            P(),
            P(),
            P(),
        ),
        out_specs=P(None, None, "lev", "lat", "lon"),
        check_vma=False,
    )
```

```python
import functools

import jax
import jax.numpy as jnp
from jax import lax
from jax.experimental import pallas as pl
from jax.experimental.pallas import tpu as pltpu
from jax.sharding import PartitionSpec as P

MESH = pl.DeviceIdType.MESH
PLUS_WEIGHTS = (-2.0, 15.0, -60.0, 20.0, 30.0, -3.0)
MINUS_WEIGHTS = (3.0, -30.0, -20.0, 60.0, -15.0, 2.0)
VMEM_LIMIT = 60 * 1024 * 1024
WIDTH = 3
SUB = 8
STEP = 22
SUM_SPAN = 16
PACK_SPAN = 16
LANES = 128


def split(x):
    hi = x.astype(jnp.bfloat16)
    lo = (x - hi.astype(jnp.float32)).astype(jnp.bfloat16)
    return hi, lo


def taper_of(r2):
    inv = lax.rsqrt(jnp.maximum(r2, 1e-30))
    r = r2 * inv
    inner = 1.0 + r2 * (-5.0 / 3.0 + r * (0.625 + r * (0.5 - 0.25 * r)))
    outer = (
        4.0
        - (2.0 / 3.0) * inv
        + r * (-5.0 + r * (5.0 / 3.0 + r * (0.625 + r * (-0.5 + r * (1.0 / 12.0)))))
    )
    return jnp.where(r2 <= 1.0, inner, jnp.where(r2 < 4.0, outer, 0.0))


def dot(a, b):
    return jnp.dot(a, b, preferred_element_type=jnp.float32)


def innovation(prior, value, err):
    members = prior.shape[0]
    centre = jnp.sum(prior, axis=0, keepdims=True) * (1.0 / members)
    spread = prior - centre
    variance = jnp.sum(spread * spread, axis=0, keepdims=True) * (1.0 / (members - 1))
    denominator = variance + err
    factor = 1.0 / (1.0 + jnp.sqrt(err / denominator))
    gain = (value - centre - factor * spread) / denominator
    return spread, gain


def spread_operand(spread):
    members, count = spread.shape
    hi, lo = split(spread * (1.0 / (members - 1)))
    pad = jnp.zeros((256 - 3 * members, count), jnp.float32)
    stacked = jnp.concatenate(
        [hi.astype(jnp.float32), lo.astype(jnp.float32), hi.astype(jnp.float32), pad], axis=0
    )
    return stacked.T.astype(jnp.bfloat16)


def anomaly_operand(x):
    members = x.shape[0]
    a = x - jnp.sum(x, axis=0, keepdims=True) * (1.0 / members)
    hi, lo = split(a)
    pad = jnp.zeros((256 - 3 * members, x.shape[1]), jnp.bfloat16)
    return jnp.concatenate([hi, hi, lo, pad], axis=0)


def apply_gain(gain_stack, gain_hi, weighted):
    members = gain_hi.shape[0]
    hi, lo = split(weighted)
    both = dot(gain_stack, hi)
    return both[:members] + both[members:] + dot(gain_hi, lo)


def kernel(
    dims,
    x_ref, cour_ref, value_ref, err_ref, owner_ref, columns_ref, out_ref,
    cand, rs_buf, z_buf, full, prior_buf,
    s_op, g_op, lon_part, row_part, col_part, taper_buf,
    state, packed, left_in, right_in, lhs, dpm, coef, stencil, picker, slot_mask, result_buf,
    load_sem, store_sem, share_send, share_recv, lat_send, lat_recv, lon_send, lon_recv,
):
    n_lon, n_lat, n_lev = dims
    members, fields, _, rows, cols = x_ref.shape
    batches, count = value_ref.shape
    total = fields * members
    lon = lax.axis_index("lon")
    lat = lax.axis_index("lat")
    lev = lax.axis_index("lev")
    has_up = lat > 0
    has_down = lat < n_lat - 1
    east = lax.rem(lon + 1, n_lon)
    west = lax.rem(lon + n_lon - 1, n_lon)
    other_lev = 1 - lev
    slot = 2 * WIDTH
    per = members // n_lat

    def load_start(f):
        def one(i, carry):
            pltpu.make_async_copy(
                x_ref.at[:, f, 0, i],
                state.at[0, WIDTH + i, pl.ds(f * members, members)],
                load_sem.at[f],
            ).start()
            return carry

        lax.fori_loop(0, rows, one, 0)

    def load_wait(f):
        view = state.at[0, pl.ds(WIDTH, rows), pl.ds(f * members, members)]
        pltpu.make_async_copy(view, view, load_sem.at[f]).wait()

    for f in range(fields):
        load_start(f)

    barrier = pltpu.get_barrier_semaphore()

    def greet_lat(t, carry):
        other = lax.rem(lat + t, n_lat)
        for v in range(2):
            pl.semaphore_signal(
                barrier, inc=1, device_id=(lon, other, (lev, other_lev)[v]), device_id_type=MESH
            )
        return carry

    def greet_lon(t, carry):
        pl.semaphore_signal(
            barrier, inc=1, device_id=(lax.rem(lon + t, n_lon), lat, lev), device_id_type=MESH
        )
        return carry

    pl.semaphore_signal(barrier, inc=1, device_id=(lon, lat, other_lev), device_id_type=MESH)
    lax.fori_loop(1, n_lat, greet_lat, 0)
    lax.fori_loop(1, n_lon, greet_lon, 0)

    lat0 = lat * rows
    lon0 = lon * cols
    n_total = cols * n_lon
    me = (lon * n_lat + lat) * n_lev + lev
    local, obs_row, obs_col = [], [], []
    for b in range(batches):
        owner = owner_ref[b]
        columns = columns_ref[b : b + 1]
        local.append(columns + jnp.where(owner == me, 0, n_total * rows * n_lat))
        obs_row.append(owner // n_lev % n_lat * rows + columns // cols)
        obs_col.append(owner // (n_lat * n_lev) * cols + columns % cols)

    @pl.when(jnp.logical_not(has_up))
    def _():
        for s in range(3):
            state[s, 0:WIDTH] = jnp.zeros((WIDTH, total, cols), jnp.float32)

    @pl.when(jnp.logical_not(has_down))
    def _():
        for s in range(3):
            state[s, rows + WIDTH :] = jnp.zeros((WIDTH, total, cols), jnp.float32)

    load_wait(0)

    picked = None
    for pair in range(rows // 2):
        parts = [state[0, WIDTH + 2 * pair + j, 0:members] for j in range(2)]
        x0 = jnp.concatenate(parts, axis=1)
        hi = x0.astype(jnp.bfloat16)
        rest = x0 - hi.astype(jnp.float32)
        mid, lo = split(rest)
        cell = lax.broadcasted_iota(jnp.int32, (2 * cols, count), 0) + pair * 2 * cols
        hot = [
            jnp.where(cell == local[b], 1.0, 0.0).astype(jnp.bfloat16)
            for b in range(batches)
        ]
        term = dot(jnp.concatenate([hi, mid, lo], axis=0), jnp.concatenate(hot, axis=1))
        picked = term if picked is None else picked + term
    picked = picked[:members] + (picked[members : 2 * members] + picked[2 * members :])
    halves = count // LANES
    for b in range(batches):
        for p in range(n_lat):
            for h in range(halves):
                at = b * count + h * LANES
                cand[b, p, h * per : (h + 1) * per] = picked[p * per : (p + 1) * per, at : at + LANES]

    for f in range(1, fields):
        load_wait(f)
    pl.semaphore_wait(barrier, 2 * n_lat + n_lon - 2)

    def field_slice(c):
        return pl.ds(pl.multiple_of(c * members, 16), members)

    def block(i):
        return pl.ds(pl.multiple_of(i * members, 16), members)

    def lat_copy(section, c, down):
        src = rows if down else WIDTH
        dst = 0 if down else WIDTH + rows
        return pltpu.make_async_remote_copy(
            src_ref=state.at[section, pl.ds(src, WIDTH), field_slice(c)],
            dst_ref=state.at[section, pl.ds(dst, WIDTH), field_slice(c)],
            send_sem=lat_send.at[section, c, int(down)],
            recv_sem=lat_recv.at[section, c, int(down)],
            device_id=(lon, lat + 1 if down else lat - 1, lev),
            device_id_type=MESH,
        )

    def lat_start(section, c):
        @pl.when(has_up)
        def _():
            lat_copy(section, c, False).start()

        @pl.when(has_down)
        def _():
            lat_copy(section, c, True).start()

    def lat_wait(section, c):
        @pl.when(has_up)
        def _():
            lat_copy(section, c, True).wait_recv()

        @pl.when(has_down)
        def _():
            lat_copy(section, c, False).wait_recv()

    def lat_sent(section, c):
        @pl.when(has_up)
        def _():
            lat_copy(section, c, False).wait_send()

        @pl.when(has_down)
        def _():
            lat_copy(section, c, True).wait_send()

    def lon_copy(section, c, to_east):
        return pltpu.make_async_remote_copy(
            src_ref=packed.at[section, field_slice(c)],
            dst_ref=(left_in if to_east else right_in).at[section, field_slice(c)],
            send_sem=lon_send.at[section, c, int(to_east)],
            recv_sem=lon_recv.at[section, c, int(to_east)],
            device_id=(east if to_east else west, lat, lev),
            device_id_type=MESH,
        )

    def wait_all(buf, number, sem):
        view = buf.at[pl.ds(0, number)]
        pltpu.make_async_copy(view, view, sem).wait()

    def piece(other, to_lev, sem):
        pltpu.make_async_remote_copy(
            src_ref=cand.at[to_lev, other], dst_ref=rs_buf.at[lev, lat],
            send_sem=share_send.at[sem], recv_sem=share_recv.at[sem],
            device_id=(lon, other, to_lev), device_id_type=MESH,
        ).start()

    def send_piece(t, carry):
        other = lax.rem(lat + t, n_lat)
        piece(other, lev, 1)
        piece(other, other_lev, 0)
        return carry

    def send_sum(t, carry):
        pltpu.make_async_remote_copy(
            src_ref=z_buf.at[lon], dst_ref=z_buf.at[lon],
            send_sem=share_send.at[2], recv_sem=share_recv.at[2],
            device_id=(lax.rem(lon + t, n_lon), lat, lev), device_id_type=MESH,
        ).start()
        return carry

    def result(other, to_lev, sem):
        pltpu.make_async_remote_copy(
            src_ref=full.at[lev, lat], dst_ref=full.at[lev, lat],
            send_sem=share_send.at[sem], recv_sem=share_recv.at[sem],
            device_id=(lon, other, to_lev), device_id_type=MESH,
        ).start()

    def send_total(t, carry):
        other = lax.rem(lat + t, n_lat)
        result(other, lev, 3)
        result(other, other_lev, 4)
        return carry

    def lon_sq(gap):
        gap = jnp.abs(gap)
        gap = jnp.minimum(gap, n_total - gap) * (1.0 / (n_total // 2))
        return gap * gap

    wide = rows + 2 * WIDTH

    def tapers(first, last):
        def one(n, carry):
            b = n // wide
            i = lax.rem(n, wide)
            here = (lat0 + i - WIDTH).astype(jnp.float32)
            for at in range(0, count, 64):
                sl = pl.ds(at, 64)
                dlat = (here - row_part[b, sl]) * (1.0 / (2.0 * rows))
                taper_buf[b, i, sl] = taper_of(dlat * dlat + lon_part[b, sl])
            return carry

        lax.fori_loop(first, last, one, 0)

    piece(lat, other_lev, 0)
    lax.fori_loop(1, n_lat, send_piece, 0)
    lat_start(0, 0)
    rs_buf[lev, lat] = cand[lev, lat]
    for b in range(batches):
        grid_cols = (lon0 + lax.broadcasted_iota(jnp.int32, (count, cols), 1)).astype(jnp.float32)
        wide_col = jnp.broadcast_to(obs_col[b].astype(jnp.float32), (cols, count)).T
        col_part[b] = wide_col
        lon_part[b] = lon_sq(grid_cols - wide_col)
        row_part[b] = jnp.broadcast_to(obs_row[b].astype(jnp.float32), (cols, count)).T
    tapers(0, 16)
    wait_all(rs_buf.at[lev], n_lat - 1, share_recv.at[1])
    wait_all(rs_buf.at[other_lev], n_lat, share_recv.at[0])
    z_buf[lon] = jnp.sum(rs_buf[0], axis=0) + jnp.sum(rs_buf[1], axis=0)
    lax.fori_loop(1, n_lon, send_sum, 0)
    lat_start(0, 1)
    tapers(16, 28)
    wait_all(z_buf, n_lon - 1, share_recv.at[2])
    full[lev, lat] = jnp.sum(z_buf[...], axis=0)
    result(lat, other_lev, 4)
    lax.fori_loop(1, n_lat, send_total, 0)
    lat_start(0, 2)
    tapers(28, 2 * wide)

    for r in range(rows):
        for d in range(2):
            c = jnp.broadcast_to(cour_ref[d, r : r + 1], (SUB, cols))
            up = jnp.maximum(c, 0.0) * (-1.0 / 60.0)
            dn = jnp.minimum(c, 0.0) * (-1.0 / 60.0)
            if d == 0:
                coef[r, 0] = up
                coef[r, 1] = dn
            else:
                for o in range(7):
                    w = PLUS_WEIGHTS[o] * up if o < 6 else jnp.zeros_like(c)
                    if o > 0:
                        w = w + MINUS_WEIGHTS[o - 1] * dn
                    coef[r, 2 + o] = w

    k = lax.broadcasted_iota(jnp.int32, (4 * cols, cols), 0)
    j = lax.broadcasted_iota(jnp.int32, (4 * cols, cols), 1)
    kk = lax.rem(k, cols)
    side = lax.rem(kk, slot)
    halo_col = jnp.where(side < WIDTH, side - WIDTH, cols + side - WIDTH)
    gap = jnp.where(k < 2 * cols, kk, halo_col) - j
    for first, weights, lane0 in ((-3, PLUS_WEIGHTS, 0), (-2, MINUS_WEIGHTS, cols)):
        w = jnp.zeros((4 * cols, cols), jnp.float32)
        for n in range(6):
            w = jnp.where(gap == first + n, weights[n], w)
        stencil[:, lane0 : lane0 + cols] = w.astype(jnp.bfloat16)
    side = lax.rem(j, slot)[: 2 * cols]
    wanted = jnp.where(side < WIDTH, cols - WIDTH + side, side - WIDTH)
    hit = (wanted == kk[: 2 * cols]) & (j[: 2 * cols] < slot * rows)
    picker[...] = jnp.where(hit, 1.0, 0.0).astype(jnp.bfloat16)

    lane = lax.broadcasted_iota(jnp.int32, (members, cols), 1)
    from_left = lax.rem(lane, slot) < WIDTH
    slot_of = lane // slot
    for r in range(rows):
        slot_mask[r] = jnp.where(slot_of == r, 1.0, 0.0).astype(jnp.bfloat16)

    wait_all(full.at[lev], n_lat - 1, share_recv.at[3])
    wait_all(full.at[other_lev], n_lat, share_recv.at[4])
    for b in range(batches):
        for p in range(n_lat):
            for h in range(halves):
                at = h * LANES
                prior_buf[b, p * per : (p + 1) * per, at : at + LANES] = full[
                    b, p, h * per : (h + 1) * per
                ]

    prior = prior_buf[0]
    for b in range(batches):
        spread, gain = innovation(prior, value_ref[b : b + 1], err_ref[b : b + 1])
        s_op[b] = spread_operand(spread)
        ghi, glo = split(gain)
        g_op[b] = jnp.concatenate([ghi, glo], axis=0)
        if b + 1 < batches:
            prior = prior_buf[b + 1]
            both = [jnp.concatenate([v[b]] * halves, axis=1) for v in (row_part, col_part)]
            dlat = (obs_row[b + 1].astype(jnp.float32) - both[0]) * (1.0 / (2.0 * rows))
            taper = taper_of(dlat * dlat + lon_sq(obs_col[b + 1].astype(jnp.float32) - both[1]))
            cov = dot(s_op[b], anomaly_operand(prior))
            prior = prior + apply_gain(g_op[b], ghi, taper * cov)

    def assimilate(c):
        def step(n, carry):
            at = [n * STEP + j for j in range(STEP)]
            x = [state[0, i, field_slice(c)] for i in at]
            for b in range(batches):
                operand = jnp.concatenate([anomaly_operand(v) for v in x], axis=1)
                cov = dot(s_op[b], operand)
                weighted = jnp.concatenate(
                    [
                        taper_buf[b, i] * cov[:, j * cols : (j + 1) * cols]
                        for j, i in enumerate(at)
                    ],
                    axis=1,
                )
                change = apply_gain(g_op[b], g_op[b, :members], weighted)
                x = [v + change[:, j * cols : (j + 1) * cols] for j, v in enumerate(x)]
            for i, v in zip(at, x):
                state[0, i, field_slice(c)] = v
                hi, lo = split(v)
                lhs[c, block(i), 0:cols] = hi
                lhs[c, block(i), cols : 2 * cols] = lo
            return carry

        lax.fori_loop(0, wide // STEP, step, 0)


    def lon_start(section, c):
        def step(n, acc):
            at = pl.multiple_of((WIDTH + n * PACK_SPAN) * members, 16)
            got = dot(lhs[c, pl.ds(at, PACK_SPAN * members), 0 : 2 * cols], picker[...])
            for m in range(PACK_SPAN):
                acc = jnp.where(slot_of == n * PACK_SPAN + m, got[m * members : (m + 1) * members], acc)
            return acc

        zero = jnp.zeros((members, cols), jnp.float32)
        packed[section, field_slice(c)] = lax.fori_loop(0, rows // PACK_SPAN, step, zero)
        lon_copy(section, c, True).start()
        lon_copy(section, c, False).start()

    def lon_finish(section, c):
        lon_copy(section, c, True).wait_recv()
        lon_copy(section, c, False).wait_recv()
        halo = jnp.where(
            from_left, left_in[section, field_slice(c)], right_in[section, field_slice(c)]
        )

        parts = split(halo)

        def step(n, carry):
            for m in range(SUM_SPAN):
                r = n * SUM_SPAN + m
                for p in range(2):
                    lanes = slice((2 + p) * cols, (3 + p) * cols)
                    lhs[c, block(WIDTH + r), lanes] = parts[p] * slot_mask[r]
            at = pl.multiple_of((WIDTH + n * SUM_SPAN) * members, 16)
            to = pl.multiple_of(n * SUM_SPAN * members, 16)
            rows_in = pl.ds(at, SUM_SPAN * members)
            dpm[pl.ds(to, SUM_SPAN * members)] = dot(lhs[c, rows_in], stencil[...])
            return carry

        lax.fori_loop(0, rows // SUM_SPAN, step, 0)

    def do_rows(section, c, first, stop):
        scale = (1.0 / 3.0, 0.5, 1.0)[section]

        def do_row(n, carry):
            r = n if isinstance(first, int) else first(n)
            w = [jnp.concatenate([coef[r, o]] * 2, axis=0) for o in range(9)]
            for g in range(members // (2 * SUB)):
                off = g * 2 * SUB
                sl = pl.ds(pl.multiple_of(c * members + off, 2 * SUB), 2 * SUB)
                at = pl.ds(pl.multiple_of(r * members + off, 2 * SUB), 2 * SUB)
                q = state[section, WIDTH + r, sl]
                t = w[0] * dpm[at, 0:cols]
                u = w[1] * dpm[at, cols : 2 * cols] + w[5] * q
                for o in (1, 2, 3):
                    t = t + w[5 - o] * state[section, WIDTH + r - o, sl]
                    u = u + w[5 + o] * state[section, WIDTH + r + o, sl]
                base = q if section == 0 else state[0, WIDTH + r, sl]
                if section < 2:
                    value = base + (t + u) * scale
                    state[section + 1, WIDTH + r, sl] = value
                    hi, lo = split(value)
                    to = pl.ds(pl.multiple_of((WIDTH + r) * members + off, 2 * SUB), 2 * SUB)
                    lhs[c, to, 0:cols] = hi
                    lhs[c, to, cols : 2 * cols] = lo
                else:
                    result_buf[r, sl] = base + (t + u)
            return carry

        lax.fori_loop(first if isinstance(first, int) else 0, stop, do_row, 0)

    def store_row(c, r):
        pltpu.make_async_copy(
            result_buf.at[r, field_slice(c)], x_out(c, r), store_sem.at[c]
        ).start()

    def x_out(c, r):
        return out_ref.at[:, c, 0, r]

    def store_wait(c):
        view = result_buf.at[:, field_slice(c)]
        pltpu.make_async_copy(view, view, store_sem.at[c]).wait()

    def interior(section, c):
        do_rows(section, c, WIDTH, rows - WIDTH)

    def edges(section, c):
        def edge_row(n):
            return jnp.where(n < WIDTH, n, n + rows - 2 * WIDTH)

        do_rows(section, c, edge_row, 2 * WIDTH)

    def first_pass(c, carry):
        @pl.when(c < fields)
        def _():
            lat_wait(0, c)
            lat_sent(0, c)
            assimilate(c)
            lon_start(0, c)

        @pl.when(c > 0)
        def _():
            lon_finish(0, c - 1)
            edges(0, c - 1)
            lat_start(1, c - 1)
            interior(0, c - 1)
            lon_start(1, c - 1)

        return carry

    lax.fori_loop(0, fields + 1, first_pass, 0)

    for section in (1, 2):

        def later_pass(c, carry):
            lon_finish(section, c)
            interior(section, c)
            if section == 2:
                for r in range(WIDTH, rows - WIDTH):
                    store_row(c, r)
            lat_wait(section, c)
            edges(section, c)
            if section == 2:
                for r in list(range(WIDTH)) + list(range(rows - WIDTH, rows)):
                    store_row(c, r)
            if section < 2:
                lat_start(section + 1, c)
                lon_start(section + 1, c)
            return carry

        lax.fori_loop(0, fields, later_pass, 0)

    for c in range(fields):
        store_wait(c)
    wait_all(rs_buf.at[lev], n_lat - 1, share_send.at[1])
    wait_all(rs_buf.at[other_lev], n_lat, share_send.at[0])
    wait_all(z_buf, n_lon - 1, share_send.at[2])
    wait_all(full.at[lev], n_lat - 1, share_send.at[3])
    wait_all(full.at[other_lev], n_lat, share_send.at[4])
    for section in range(3):
        for c in range(fields):
            lon_copy(section, c, True).wait_send()
            lon_copy(section, c, False).wait_send()
            if section > 0:
                lat_sent(section, c)


def on_device(ensemble, courant, obs_value, obs_error, owner_device, columns):
    members, fields, _, rows, cols = ensemble.shape
    dims = tuple(lax.axis_size(a) for a in ("lon", "lat", "lev"))
    n_lon, n_lat, _ = dims
    batches, count = columns.shape
    total = fields * members
    piece = (members // n_lat * count // LANES, LANES)
    f32, bf16 = jnp.float32, jnp.bfloat16
    vmem = pl.BlockSpec(memory_space=pltpu.VMEM)
    smem = pl.BlockSpec(memory_space=pltpu.SMEM)
    dma = pltpu.SemaphoreType.DMA
    out = pl.pallas_call(
        functools.partial(kernel, dims),
        out_shape=jax.ShapeDtypeStruct(ensemble.shape, f32),
        in_specs=[pl.BlockSpec(memory_space=pl.ANY)] + [vmem] * 3 + [smem, vmem],
        out_specs=pl.BlockSpec(memory_space=pl.ANY),
        scratch_shapes=[
            pltpu.VMEM((batches, n_lat) + piece, f32),
            pltpu.VMEM((batches, n_lat) + piece, f32),
            pltpu.VMEM((n_lon,) + piece, f32),
            pltpu.VMEM((batches, n_lat) + piece, f32),
            pltpu.VMEM((batches, members, count), f32),
            pltpu.VMEM((batches, count, 256), bf16),
            pltpu.VMEM((batches, 2 * members, count), bf16),
            pltpu.VMEM((batches, count, cols), f32),
            pltpu.VMEM((batches, count, cols), f32),
            pltpu.VMEM((batches, count, cols), f32),
            pltpu.VMEM((batches, rows + 2 * WIDTH, count, cols), f32),
            pltpu.VMEM((3, rows + 2 * WIDTH, total, cols), f32),
            pltpu.VMEM((3, total, cols), f32),
            pltpu.VMEM((3, total, cols), f32),
            pltpu.VMEM((3, total, cols), f32),
            pltpu.VMEM((fields, (rows + 2 * WIDTH) * members, 4 * cols), bf16),
            pltpu.VMEM((rows * members, 2 * cols), f32),
            pltpu.VMEM((rows, 9, SUB, cols), f32),
            pltpu.VMEM((4 * cols, 2 * cols), bf16),
            pltpu.VMEM((2 * cols, cols), bf16),
            pltpu.VMEM((rows, members, cols), bf16),
            pltpu.VMEM((rows, total, cols), f32),
            dma((fields,)),
            dma((fields,)),
            dma((5,)),
            dma((5,)),
            dma((3, fields, 2)),
            dma((3, fields, 2)),
            dma((3, fields, 2)),
            dma((3, fields, 2)),
        ],
        compiler_params=pltpu.CompilerParams(
            has_side_effects=True, collective_id=0, vmem_limit_bytes=VMEM_LIMIT
        ),
        name="filter_and_advect",
    )(
        ensemble, courant[:, 0], obs_value, obs_error, owner_device, columns,
    )
    return out


def solution(mesh):
    return jax.shard_map(
        on_device,
        mesh=mesh,
        in_specs=(
            P(None, None, "lev", "lat", "lon"),
            P(None, "lev", "lat", "lon"),
            P(),
            P(),
            P(),
            P(),
        ),
        out_specs=P(None, None, "lev", "lat", "lon"),
        check_vma=False,
    )
```
